512 devices in a mesh: patch: 128 (over z, y_hi, x), batch: 4 (over y_lo, core).
Axes of the slice: x: 4, y: 4 (y_hi: 2, y_lo: 2; y = y_hi * 2 + y_lo), z: 16, core: 2. Of those that a mesh axis runs over, the one named last changes fastest.
Arguments:
- block_input: bfloat16 [128, 128, 640], P('patch', 'batch'), parts along dimension 1, may hold values from -6 to 6
- stale_input: bfloat16 [128, 128, 640], P('patch', 'batch'), parts along dimension 1, may hold values from -6 to 6
- query_weight: bfloat16 [640, 640], replicated, may hold values from -5 to 5
- key_weight: bfloat16 [640, 640], replicated, may hold values from -0.25 to 0.25
- value_weight: bfloat16 [640, 640], replicated, may hold values from -0.25 to 0.25
- out_weight: bfloat16 [640, 640], replicated, may hold values from -0.25 to 0.25
- conv_weight: bfloat16 [9, 640, 320], P(None, 'patch'), may hold values from -0.078125 to 0.078125
Outputs:
- attended: bfloat16 [128, 128, 640], P('patch', 'batch'), parts along dimension 1
- convolved: bfloat16 [128, 128, 320], P('patch', 'batch'), parts along dimension 1
The draws below stay inside these ranges and needn't reach their ends.
There are 4 independent parts, one for each index of `batch`. The reference program is written for one: setup_inputs(seed, part) draws one part's arguments, and reference() takes and returns one part's arrays. A program takes and returns all parts, laid end to end along the dimension named above; an argument that names none is the same for every part. Nothing has to cross between parts.
All inputs are finite; a program needn't handle non-finite values.
Results may differ from the reference program's by a relative error of at most 0.009.
The reference program's roundings to bfloat16 on the way count: a program that leaves them out, or rounds other values in their place, can miss the bound.
Values may be sent and summed in bfloat16 or wider, within the bound.
No kernel may reach another device: no remote copies, remote signals or barrier semaphores. Data moves between devices by JAX's collectives and lax.ppermute only.
A program may use at most 64 MiB of HBM per device.

```python
import jax
import jax.numpy as jnp
from jax import lax

D = 640
HEADS = 10
HEAD_DIM = 64
CO = 320
COLS = 32
ROWS = 128


def draw_query_weight(key, part):
    key = jax.random.fold_in(key, 11)
    spread = 3.0
    normal_part = jnp.clip(jax.random.normal(key, (D, HEADS * HEAD_DIM), jnp.float32), -4.0, 4.0)
    scaled = jnp.clip(normal_part * (spread / D ** 0.5), -5.0, 5.0)
    return scaled.astype(jnp.bfloat16)


def shard_levels(key, shape, split, low, top_value):
    gain = 1.0
    for position, blocks in split:
        steps = jax.random.uniform(jax.random.fold_in(jax.random.fold_in(key, 6), position), (blocks,), jnp.float32, low / len(split), top_value / len(split))
        gain = gain * jnp.repeat(jnp.exp(steps), shape[position] // blocks).reshape((-1,) + (1,) * (len(shape) - 1 - position))
    return gain


def noise(rng, extent, scale, limit, split=(), kind=jnp.bfloat16):
    gain = shard_levels(rng, extent, split, -0.22, 0.18) if split else 1.0
    entries = jax.random.normal(rng, extent, jnp.float32) * scale * gain
    return jnp.minimum(jnp.maximum(entries, -limit), limit).astype(kind)


def setup_inputs(seed: int = 0, part: int = 0) -> dict:
    keys = jax.random.split(jax.random.key(seed), 8)
    part_keys = jax.random.split(jax.random.fold_in(keys[7], part), 8)
    block_input = noise(part_keys[0], (ROWS, COLS, D), 1.0, 6.0, ((0, 128),))
    stale_input = noise(part_keys[1], (ROWS, COLS, D), 1.0, 6.0, ((0, 128),))
    query_weight = draw_query_weight(jax.random.fold_in(keys[7], 71), part)
    key_weight = noise(keys[3], (D, HEADS * HEAD_DIM), D ** -0.5, 0.25)
    value_weight = noise(keys[4], (D, HEADS * HEAD_DIM), D ** -0.5, 0.25)
    out_weight = noise(keys[5], (HEADS * HEAD_DIM, D), (HEADS * HEAD_DIM) ** -0.5, 0.25)
    conv_weight = noise(keys[6], (9, D, CO), (9 * D) ** -0.5, 0.078125, ((1, 128),))
    return dict(block_input=block_input, stale_input=stale_input, query_weight=query_weight, key_weight=key_weight, value_weight=value_weight, out_weight=out_weight, conv_weight=conv_weight)


def layer_norm(values_in):
    mean = lax.optimization_barrier(jnp.mean(values_in, axis=-1, keepdims=True))
    centered = values_in - mean
    variance = lax.optimization_barrier(jnp.mean(centered * centered, axis=-1, keepdims=True))
    return centered * lax.rsqrt(variance + 1e-05)

def reference(block_input, stale_input, query_weight, key_weight, value_weight, out_weight, conv_weight):
    strips, columns, channels = block_input.shape
    tokens_flat = block_input.reshape(strips * columns, channels)
    stale_flat = stale_input.reshape(strips * columns, channels)
    normed = layer_norm(tokens_flat.astype(jnp.float32)).astype(jnp.bfloat16)
    stale_normed = layer_norm(stale_flat.astype(jnp.float32)).astype(jnp.bfloat16)
    query = jnp.dot(normed, query_weight, preferred_element_type=jnp.float32).astype(jnp.bfloat16)
    key_fresh = jnp.dot(normed, key_weight, preferred_element_type=jnp.float32).astype(jnp.bfloat16)
    value_fresh = jnp.dot(normed, value_weight, preferred_element_type=jnp.float32).astype(jnp.bfloat16)
    key_stale = jnp.dot(stale_normed, key_weight, preferred_element_type=jnp.float32).astype(jnp.bfloat16)
    value_stale = jnp.dot(stale_normed, value_weight, preferred_element_type=jnp.float32).astype(jnp.bfloat16)
    total_keys = strips * columns

    def one_strip(strip_index):
        offset = (strip_index * columns).astype(jnp.int32)
        queries = lax.dynamic_slice_in_dim(query, offset, columns, 0).reshape(columns, HEADS, HEAD_DIM)
        key_rows = lax.dynamic_update_slice_in_dim(key_stale, lax.dynamic_slice_in_dim(key_fresh, offset, columns, 0), offset, 0)
        value_rows = lax.dynamic_update_slice_in_dim(value_stale, lax.dynamic_slice_in_dim(value_fresh, offset, columns, 0), offset, 0)
        key_rows = key_rows.reshape(total_keys, HEADS, HEAD_DIM).astype(jnp.float32)
        value_rows = value_rows.reshape(total_keys, HEADS, HEAD_DIM).astype(jnp.float32)
        scores = jnp.einsum('qhd,khd->hqk', queries.astype(jnp.float32), key_rows) * HEAD_DIM ** (-0.5)
        row_max = lax.optimization_barrier(jnp.max(scores, axis=-1, keepdims=True))
        exp_scores = jnp.exp(scores - row_max)
        row_sum = lax.optimization_barrier(jnp.sum(exp_scores, axis=-1))
        probs = exp_scores.astype(jnp.bfloat16).astype(jnp.float32)
        weighted = jnp.einsum('hqk,khd->hqd', probs, value_rows) / row_sum[:, :, None]
        return jnp.transpose(weighted, (1, 0, 2)).reshape(columns, HEADS * HEAD_DIM).astype(jnp.bfloat16)
    mixed = lax.map(one_strip, jnp.arange(strips, dtype=jnp.int32)).reshape(total_keys, HEADS * HEAD_DIM)
    attended = jnp.dot(mixed, out_weight, preferred_element_type=jnp.float32).astype(jnp.bfloat16)
    attended = attended.reshape(strips, columns, channels)
    activated = jax.nn.silu(block_input.astype(jnp.float32)).astype(jnp.bfloat16)
    stale_activated = jax.nn.silu(stale_input.astype(jnp.float32)).astype(jnp.bfloat16)
    zero_row = jnp.zeros((1, columns, channels), jnp.bfloat16)
    upper_rows = jnp.concatenate([zero_row, stale_activated[:-1]], axis=0)
    lower_rows = jnp.concatenate([stale_activated[1:], zero_row], axis=0)
    padded = jnp.stack([upper_rows, activated, lower_rows], axis=1)
    padded = jnp.pad(padded, ((0, 0), (0, 0), (1, 1), (0, 0)))
    patches = jnp.concatenate([padded[:, row_off, col_off:col_off + columns, :] for row_off in range(3) for col_off in range(3)], axis=-1)
    taps = conv_weight.reshape(9 * channels, conv_weight.shape[2])
    convolved = jnp.dot(patches.reshape(strips * columns, 9 * channels), taps, preferred_element_type=jnp.float32)
    convolved = convolved.astype(jnp.bfloat16).reshape(strips, columns, conv_weight.shape[2])
    return (attended, convolved)
```

```python
import jax
import jax.numpy as jnp
import ml_dtypes
import numpy as np
from jax import lax
from jax.experimental import pallas as pl
from jax.experimental.pallas import tpu as pltpu
from jax.sharding import Mesh, PartitionSpec as P

HEADS = 10
HEAD_DIM = 64
D = 640
CO = 320
COLS = 32
Z = 16
GROUP = 8
OWN = 5
LANES = 128
PAIRS = HEADS // 2
QUERIES = GROUP * COLS
KEYS = Z * COLS
SEND = D + 3 * LANES
BACK = D + LANES + 3 * LANES
VMEM = 24 * 1024 * 1024
F32 = jnp.float32
BF16 = jnp.bfloat16


def slice_matrix():
    out = np.zeros((D, GROUP * LANES), np.float32)
    for j in range(GROUP):
        for z in range(Z):
            for c in range(OWN):
                out[(z * GROUP + j) * OWN + c, LANES * j + 8 * z + c] = 1.0
    return out.astype(ml_dtypes.bfloat16)


def tap_matrix():
    out = np.zeros((3 * LANES, 2 * LANES), np.float32)
    for dx in range(3):
        for z in range(Z):
            for c in range(OWN):
                out[LANES * dx + 8 * z + c, 16 * z + OWN * dx + c] = 1.0
    return out.astype(ml_dtypes.bfloat16)


def layer_norm(values_in):
    mean = jnp.mean(values_in, axis=-1, keepdims=True)
    centered = values_in - mean
    variance = jnp.mean(centered * centered, axis=-1, keepdims=True)
    return (centered * lax.rsqrt(variance + 1e-05)).astype(BF16)


def silu(values_in):
    return (values_in * jax.nn.sigmoid(values_in)).astype(BF16)


def dot(a, b):
    return jnp.dot(a, b, preferred_element_type=F32)


def dot_t(a, b):
    return lax.dot_general(a, b, (((1,), (1,)), ((), ())), preferred_element_type=F32)


def lane_ids(rows):
    return lax.broadcasted_iota(jnp.int32, (rows, LANES), 1)


def prepare_kernel(ids, block, stale, halo, taps, wq, slices, send, query_out, gather, rows):
    query = dot(layer_norm(block[...].astype(F32)), wq[...]).astype(BF16)
    query = query * jnp.array(HEAD_DIM**-0.5, BF16)
    query_out[...] = query
    three = jnp.concatenate(
        [silu(block[...].astype(F32)), silu(stale[...].astype(F32)), silu(halo[...].astype(F32))],
        axis=0,
    )
    cut = dot(three, slices[...]).astype(BF16)
    for j in range(GROUP):
        send[j, :, :D] = query
        for part in range(3):
            send[j, :, D + part * LANES : D + (part + 1) * LANES] = cut[
                part * COLS : (part + 1) * COLS, j * LANES : (j + 1) * LANES
            ]
    gather[:COLS, :] = stale[...]
    core = ids[2]
    rows[...] = jnp.zeros_like(rows)
    for dx in range(3):
        first = jnp.where(core == 0, taps[dx].astype(F32), taps[6 + dx].astype(F32))
        second = jnp.where(core == 0, taps[3 + dx].astype(F32), 0.0)
        rows[OWN * dx : OWN * (dx + 1), :] = jnp.concatenate([first, second], axis=1)
    gather[COLS:, :] = rows[...].astype(BF16)


def attend_pair(query, keys, values, masked, lanes):
    low = lanes < HEAD_DIM
    zero = jnp.zeros_like(query)
    two = jnp.concatenate([jnp.where(low, query, zero), jnp.where(low, zero, query)], axis=0)
    scores = dot_t(two, keys)
    if masked is not None:
        scores = jnp.where(masked, -1e30, scores)
    row_max = jnp.max(scores, axis=-1, keepdims=True)
    exp_scores = jnp.exp(scores - row_max)
    row_sum = jnp.sum(exp_scores, axis=-1, keepdims=True)
    weighted = dot(exp_scores.astype(BF16), values)
    return row_max, row_sum, weighted


def attend_kernel(ids, sent, gathered, wk, wv, back):
    stale = gathered[:, :COLS, :].reshape(KEYS, D)
    normed = layer_norm(stale.astype(F32))
    keys = dot(normed, wk[...]).astype(BF16)
    values = dot(normed, wv[...]).astype(BF16)
    z, j = ids[0], ids[1]
    row = lax.broadcasted_iota(jnp.int32, (2 * QUERIES, KEYS), 0)
    col = lax.broadcasted_iota(jnp.int32, (2 * QUERIES, KEYS), 1)
    masked = (((row // COLS) % GROUP) == j) & ((col // COLS) == z)
    lanes = lane_ids(QUERIES)
    low = lanes < HEAD_DIM
    stats = jnp.zeros((QUERIES, LANES), F32)
    for pair in range(PAIRS):
        at = slice(pair * LANES, (pair + 1) * LANES)
        query = sent[:, :, at].reshape(QUERIES, LANES)
        row_max, row_sum, weighted = attend_pair(query, keys[:, at], values[:, at], masked, lanes)
        weighted = weighted / row_sum
        mixed = jnp.where(low, weighted[:QUERIES], weighted[QUERIES:])
        back[:, :, at] = mixed.astype(BF16).reshape(GROUP, COLS, LANES)
        for half in range(2):
            head = 2 * pair + half
            at_rows = slice(half * QUERIES, (half + 1) * QUERIES)
            stats = jnp.where(lanes == head, row_max[at_rows], stats)
            stats = jnp.where(lanes == 16 + head, row_sum[at_rows], stats)
    high = stats.astype(BF16).astype(F32)
    rest = stats - high
    middle = rest.astype(BF16).astype(F32)
    last = rest - middle
    packed = high + pltpu.roll(middle, 32, 1) + pltpu.roll(last, 64, 1)
    back[:, :, D : D + LANES] = packed.astype(BF16).reshape(GROUP, COLS, LANES)


def convolve_kernel(ids, sent, gathered, other, spread, back_in, back):
    del back_in
    core = ids[2]
    mine = gathered[:, COLS:, :].reshape(Z * 16, D)
    theirs = other[...].reshape(Z * 16, D)
    zero_core = core == 0
    lower_half = jnp.where(zero_core, mine, theirs)
    upper_half = jnp.where(zero_core, theirs, mine)
    weights = (lower_half[:, :CO], lower_half[:, CO:], upper_half[:, :CO])
    active = sent[:, :, :LANES]
    stale = sent[:, :, LANES : 2 * LANES]
    upper = jnp.concatenate([sent[7:8, :, 2 * LANES :], stale[:7]], axis=0)
    lower = jnp.concatenate([stale[1:], sent[0:1, :, 2 * LANES :]], axis=0)
    column = lax.broadcasted_iota(jnp.int32, (QUERIES, LANES), 0) % COLS
    total = jnp.zeros((QUERIES, CO), F32)
    for dy, source in enumerate((upper, active, lower)):
        rows = source.reshape(QUERIES, LANES).astype(F32)
        left = jnp.where(column == 0, 0.0, pltpu.roll(rows, 1, 0))
        right = jnp.where(column == COLS - 1, 0.0, pltpu.roll(rows, QUERIES - 1, 0))
        three = jnp.concatenate([left.astype(BF16), rows.astype(BF16), right.astype(BF16)], axis=1)
        total += dot(dot(three, spread[...]).astype(BF16), weights[dy])
    back[:, :, :CO] = total.astype(BF16).reshape(GROUP, COLS, CO)


def fresh_kernel(block, query, wk, wv, after, weighted_out, stats_out):
    del after
    normed = layer_norm(block[...].astype(F32))
    keys = dot(normed, wk[...]).astype(BF16)
    values = dot(normed, wv[...]).astype(BF16)
    lanes = lane_ids(COLS)
    low = lanes < HEAD_DIM
    stats = jnp.zeros((COLS, LANES), F32)
    for pair in range(PAIRS):
        at = slice(pair * LANES, (pair + 1) * LANES)
        row_max, row_sum, weighted = attend_pair(
            query[:, at], keys[:, at], values[:, at], None, lanes
        )
        weighted_out[:, at] = jnp.where(low, weighted[:COLS], weighted[COLS:])
        for half in range(2):
            head = 2 * pair + half
            at_rows = slice(half * COLS, (half + 1) * COLS)
            stats = jnp.where(lanes == head, row_max[at_rows], stats)
            stats = jnp.where(lanes == 16 + head, row_sum[at_rows], stats)
    stats_out[...] = stats


def finish_kernel(partial, fresh, fresh_stats, wo, attended, convolved):
    total = jnp.zeros((COLS, CO), F32)
    for d in range(GROUP):
        total += partial[d, :, D + LANES : D + LANES + CO].astype(F32)
    convolved[...] = total.astype(BF16)
    stats = []
    for d in range(GROUP):
        packed = partial[d, :, D : D + LANES].astype(F32)
        stats.append(
            packed + pltpu.roll(packed, LANES - 32, 1) + pltpu.roll(packed, LANES - 64, 1)
        )
    stats.append(fresh_stats[...])
    top = stats[0]
    for s in stats[1:]:
        top = jnp.maximum(top, s)
    scale = [jnp.exp(s - top) for s in stats]
    sums = [pltpu.roll(s, LANES - 16, 1) for s in stats]
    parts = [scale[d] * sums[d] for d in range(GROUP)]
    whole = scale[GROUP] * sums[GROUP]
    for p in parts:
        whole = whole + p
    weights = [p / whole for p in parts] + [scale[GROUP] / whole]
    low = lane_ids(COLS) < HEAD_DIM
    mixed = []
    for pair in range(PAIRS):
        at = slice(pair * LANES, (pair + 1) * LANES)
        sum_pair = jnp.zeros((COLS, LANES), F32)
        for d in range(GROUP + 1):
            w = jnp.where(
                low, weights[d][:, 2 * pair : 2 * pair + 1], weights[d][:, 2 * pair + 1 : 2 * pair + 2]
            )
            sum_pair += w * (partial[d, :, at].astype(F32) if d < GROUP else fresh[:, at])
        mixed.append(sum_pair.astype(BF16))
    attended[...] = dot(jnp.concatenate(mixed, axis=1), wo[...]).astype(BF16)


SMEM_SPEC = pl.BlockSpec(memory_space=pltpu.SMEM)
ANY_SPEC = pl.BlockSpec(memory_space=pl.ANY)


def whole(*shape):
    return pl.BlockSpec(shape, lambda i: (0,) * len(shape))


def params():
    return pltpu.CompilerParams(vmem_limit_bytes=VMEM)


def shape(dims, dtype=BF16):
    return jax.ShapeDtypeStruct(dims, dtype)


def local(block_input, stale_input, query_weight, key_weight, value_weight, out_weight, conv_weight):
    block = block_input.reshape(COLS, D)
    stale = stale_input.reshape(COLS, D)
    ids = jnp.stack(
        [lax.axis_index("z"), lax.axis_index(("yh", "x")), lax.axis_index("core")]
    ).astype(jnp.int32)
    pairs = [(GROUP * z + 7, GROUP * (z + 1) + 7) for z in range(Z - 1)]
    pairs += [(GROUP * (z + 1), GROUP * z) for z in range(Z - 1)]
    halo = lax.ppermute(stale, ("z", "yh", "x"), pairs)
    with jax.named_scope("prepare"):
        send, query, payload = pl.pallas_call(
            prepare_kernel,
            out_shape=(shape((GROUP, COLS, SEND)), shape((COLS, D)), shape((COLS + 16, D))),
            in_specs=[SMEM_SPEC] + [pl.BlockSpec(memory_space=pltpu.VMEM)] * 6,
            scratch_shapes=[pltpu.VMEM((16, D), F32)],
            compiler_params=params(),
        )(ids, block, stale, halo, conv_weight, query_weight, jnp.asarray(slice_matrix()))
    sent = lax.all_to_all(send, ("yh", "x"), 0, 0, tiled=True)
    gathered = lax.all_gather(payload, "z", axis=0)
    other = lax.ppermute(gathered[:, COLS:, :], "core", [(0, 1), (1, 0)])
    with jax.named_scope("attend"):
        back = pl.pallas_call(
            attend_kernel,
            grid=(1,),
            out_shape=shape((GROUP, COLS, BACK)),
            in_specs=[
                SMEM_SPEC,
                whole(GROUP, COLS, D),
                whole(Z, COLS + 16, D),
                whole(D, D),
                whole(D, D),
            ],
            out_specs=whole(GROUP, COLS, D + LANES),
            compiler_params=params(),
        )(ids, sent, gathered, key_weight, value_weight)
    with jax.named_scope("convolve"):
        back = pl.pallas_call(
            convolve_kernel,
            grid=(1,),
            out_shape=shape((GROUP, COLS, BACK)),
            in_specs=[
                SMEM_SPEC,
                pl.BlockSpec((pl.Element(GROUP), pl.Element(COLS), pl.Element(3 * LANES)), lambda i: (0, 0, D)),
                pl.BlockSpec((Z, COLS + 16, D), lambda i: (0, 0, 0)),
                pl.BlockSpec((Z, 16, D), lambda i: (0, 0, 0)),
                pl.BlockSpec((3 * LANES, 2 * LANES), lambda i: (0, 0)),
                ANY_SPEC,
            ],
            out_specs=pl.BlockSpec((GROUP, COLS, 3 * LANES), lambda i: (0, 0, 2)),
            input_output_aliases={5: 0},
            compiler_params=params(),
        )(ids, sent, gathered, other, jnp.asarray(tap_matrix()), back)
    partial = lax.all_to_all(back, ("yh", "x"), 0, 0, tiled=True)
    with jax.named_scope("fresh"):
        fresh, fresh_stats = pl.pallas_call(
            fresh_kernel,
            out_shape=(shape((COLS, D), F32), shape((COLS, LANES), F32)),
            in_specs=[pl.BlockSpec(memory_space=pltpu.VMEM)] * 4 + [ANY_SPEC],
            compiler_params=params(),
        )(block, query, key_weight, value_weight, back)
    with jax.named_scope("finish"):
        attended, convolved = pl.pallas_call(
            finish_kernel,
            out_shape=(shape((COLS, D)), shape((COLS, CO))),
            compiler_params=params(),
        )(partial, fresh, fresh_stats, out_weight)
    return attended.reshape(1, COLS, D), convolved.reshape(1, COLS, CO)


def solution(mesh):
    axes = Mesh(mesh.devices.reshape(Z, 2, 4, 2, 2), ("z", "yh", "x", "yl", "core"))
    rows, batch = ("z", "yh", "x"), ("yl", "core")
    placed = P(rows, batch, None)
    return jax.shard_map(
        local,
        mesh=axes,
        in_specs=(placed, placed, P(), P(), P(), P(), P(None, rows, None)),
        out_specs=(placed, placed),
        check_vma=False,
    )
```

```python
import jax
import jax.numpy as jnp
import ml_dtypes
import numpy as np
from jax import lax
from jax.experimental import pallas as pl
from jax.experimental.pallas import tpu as pltpu
from jax.sharding import Mesh, PartitionSpec as P

HEADS = 10
HEAD_DIM = 64
D = 640
CO = 320
COLS = 32
Z = 16
GROUP = 8
OWN = 5
LANES = 128
PAIRS = HEADS // 2
QUERIES = GROUP * COLS
KEYS = Z * COLS
SEND = D + 3 * LANES
BACK = D + 3 * LANES
STATS_AT = (64, 84, 104)
VMEM = 24 * 1024 * 1024
F32 = jnp.float32
BF16 = jnp.bfloat16


def slice_matrix():
    out = np.zeros((D, GROUP * LANES), np.float32)
    for j in range(GROUP):
        for z in range(Z):
            for c in range(OWN):
                out[(z * GROUP + j) * OWN + c, LANES * j + 8 * z + c] = 1.0
    return out.astype(ml_dtypes.bfloat16)


def tap_matrix():
    out = np.zeros((3 * LANES, 2 * LANES), np.float32)
    for dx in range(3):
        for z in range(Z):
            for c in range(OWN):
                out[LANES * dx + 8 * z + c, 16 * z + OWN * dx + c] = 1.0
    return out.astype(ml_dtypes.bfloat16)


def layer_norm(values_in):
    mean = jnp.mean(values_in, axis=-1, keepdims=True)
    centered = values_in - mean
    variance = jnp.mean(centered * centered, axis=-1, keepdims=True)
    return (centered * lax.rsqrt(variance + 1e-05)).astype(BF16)


def silu(values_in):
    return (values_in * jax.nn.sigmoid(values_in)).astype(BF16)


def dot(a, b):
    return jnp.dot(a, b, preferred_element_type=F32)


def dot_t(a, b):
    return lax.dot_general(a, b, (((1,), (1,)), ((), ())), preferred_element_type=F32)


def lane_ids(rows):
    return lax.broadcasted_iota(jnp.int32, (rows, LANES), 1)


def place():
    return lax.axis_index("z"), lax.axis_index("yh") * 4 + lax.axis_index("x")


def payload_kernel(stale_hbm, taps_hbm, gather, stale, taps, rows, sems):
    copies = [
        pltpu.make_async_copy(taps_hbm, taps, sems.at[0]),
        pltpu.make_async_copy(stale_hbm, stale, sems.at[1]),
    ]
    for copy in copies:
        copy.start()
    core = lax.axis_index("core")
    rows[...] = jnp.zeros_like(rows)
    copies[0].wait()
    for dx in range(3):
        first = jnp.where(core == 0, taps[dx].astype(F32), taps[6 + dx].astype(F32))
        second = jnp.where(core == 0, taps[3 + dx].astype(F32), 0.0)
        rows[OWN * dx : OWN * (dx + 1), :] = jnp.concatenate([first, second], axis=1)
    gather[COLS:, :] = rows[...].astype(BF16)
    copies[1].wait()
    gather[:COLS, :] = stale[...]


def prepare_kernel(block, gathered, wq, slices, send, query_out):
    z, j = place()
    query = dot(layer_norm(block[...].astype(F32)), wq[...]).astype(BF16)
    query = query * jnp.array(HEAD_DIM**-0.5, BF16)
    query_out[...] = query
    stale = gathered[z, :COLS, :]
    beside = jnp.where(j == 0, jnp.minimum(z + 1, Z - 1), jnp.maximum(z - 1, 0))
    outside = ((j == 0) & (z == Z - 1)) | ((j != 0) & (z == 0))
    halo = gathered[beside, :COLS, :].astype(F32) * jnp.where(outside, 0.0, 1.0)
    three = jnp.concatenate(
        [silu(block[...].astype(F32)), silu(stale.astype(F32)), silu(halo)], axis=0
    )
    cut = dot(three, slices[...]).astype(BF16)
    for j in range(GROUP):
        send[j, :, :D] = query
        for part in range(3):
            send[j, :, D + part * LANES : D + (part + 1) * LANES] = cut[
                part * COLS : (part + 1) * COLS, j * LANES : (j + 1) * LANES
            ]


def project_kernel(gathered, wk, wv, after, keys, values):
    del after
    normed = layer_norm(gathered[:, :COLS, :].reshape(KEYS, D).astype(F32))
    keys[...] = dot(normed, wk[...]).astype(BF16)
    values[...] = dot(normed, wv[...]).astype(BF16)


def attend_pair(query, keys, values, masked, lanes):
    low = lanes < HEAD_DIM
    zero = jnp.zeros_like(query)
    two = jnp.concatenate([jnp.where(low, query, zero), jnp.where(low, zero, query)], axis=0)
    scores = dot_t(two, keys)
    if masked is not None:
        scores = jnp.where(masked, -1e30, scores)
    row_max = jnp.max(scores, axis=-1, keepdims=True)
    exp_scores = jnp.exp(scores - row_max)
    row_sum = jnp.sum(exp_scores, axis=-1, keepdims=True)
    weighted = dot(exp_scores.astype(BF16), values)
    return row_max, row_sum, weighted


def convolve(sent, gathered, other, spread):
    mine = gathered[:, COLS:, :].reshape(Z * 16, D)
    theirs = other[...].reshape(Z * 16, D)
    zero_core = lax.axis_index("core") == 0
    lower_half = jnp.where(zero_core, mine, theirs)
    upper_half = jnp.where(zero_core, theirs, mine)
    weights = (lower_half[:, :CO], lower_half[:, CO:], upper_half[:, :CO])
    active = sent[:, :, D : D + LANES]
    stale = sent[:, :, D + LANES : D + 2 * LANES]
    upper = jnp.concatenate([sent[7:8, :, D + 2 * LANES :], stale[:7]], axis=0)
    lower = jnp.concatenate([stale[1:], sent[0:1, :, D + 2 * LANES :]], axis=0)
    column = lax.broadcasted_iota(jnp.int32, (QUERIES, LANES), 0) % COLS
    total = jnp.zeros((QUERIES, CO), F32)
    for dy, source in enumerate((upper, active, lower)):
        rows = source.reshape(QUERIES, LANES).astype(F32)
        left = jnp.where(column == 0, 0.0, pltpu.roll(rows, 1, 0))
        right = jnp.where(column == COLS - 1, 0.0, pltpu.roll(rows, QUERIES - 1, 0))
        three = jnp.concatenate([left.astype(BF16), rows.astype(BF16), right.astype(BF16)], axis=1)
        total += dot(dot(three, spread[...]).astype(BF16), weights[dy])
    return total


def attend_kernel(sent, keys, values, gathered, other, spread, back):
    z, j = place()
    row = lax.broadcasted_iota(jnp.int32, (2 * QUERIES, KEYS), 0)
    col = lax.broadcasted_iota(jnp.int32, (2 * QUERIES, KEYS), 1)
    masked = (((row // COLS) % GROUP) == j) & ((col // COLS) == z)
    lanes = lane_ids(QUERIES)
    low = lanes < HEAD_DIM
    stats = jnp.zeros((QUERIES, LANES), F32)
    for pair in range(PAIRS):
        at = slice(pair * LANES, (pair + 1) * LANES)
        query = sent[:, :, at].reshape(QUERIES, LANES)
        row_max, row_sum, weighted = attend_pair(query, keys[:, at], values[:, at], masked, lanes)
        weighted = weighted / row_sum
        mixed = jnp.where(low, weighted[:QUERIES], weighted[QUERIES:])
        back[:, :, at] = mixed.astype(BF16).reshape(GROUP, COLS, LANES)
        for half in range(2):
            head = 2 * pair + half
            at_rows = slice(half * QUERIES, (half + 1) * QUERIES)
            stats = jnp.where(lanes == head, row_max[at_rows], stats)
            stats = jnp.where(lanes == HEADS + head, row_sum[at_rows], stats)
    high = stats.astype(BF16).astype(F32)
    rest = stats - high
    middle = rest.astype(BF16).astype(F32)
    last = rest - middle
    packed = sum(pltpu.roll(term, at, 1) for term, at in zip((high, middle, last), STATS_AT))
    total = convolve(sent, gathered, other, spread)
    back[:, :, D : D + 2 * LANES] = (
        total[:, : 2 * LANES].astype(BF16).reshape(GROUP, COLS, 2 * LANES)
    )
    tail = jnp.concatenate([total[:, 2 * LANES :], packed[:, CO - 2 * LANES :]], axis=1)
    back[:, :, D + 2 * LANES :] = tail.astype(BF16).reshape(GROUP, COLS, LANES)


def fresh_kernel(block, query, wk, wv, after, weighted_out, stats_out):
    del after
    normed = layer_norm(block[...].astype(F32))
    keys = dot(normed, wk[...]).astype(BF16)
    values = dot(normed, wv[...]).astype(BF16)
    lanes = lane_ids(COLS)
    low = lanes < HEAD_DIM
    stats = jnp.zeros((COLS, LANES), F32)
    for pair in range(PAIRS):
        at = slice(pair * LANES, (pair + 1) * LANES)
        row_max, row_sum, weighted = attend_pair(
            query[:, at], keys[:, at], values[:, at], None, lanes
        )
        weighted_out[:, at] = jnp.where(low, weighted[:COLS], weighted[COLS:])
        for half in range(2):
            head = 2 * pair + half
            at_rows = slice(half * COLS, (half + 1) * COLS)
            stats = jnp.where(lanes == head, row_max[at_rows], stats)
            stats = jnp.where(lanes == HEADS + head, row_sum[at_rows], stats)
    stats_out[...] = stats


def finish_kernel(partial, fresh, fresh_stats, wo, attended, convolved):
    total = jnp.zeros((COLS, CO), F32)
    for d in range(GROUP):
        total += partial[d, :, D : D + CO].astype(F32)
    convolved[...] = total.astype(BF16)
    stats = []
    for d in range(GROUP):
        packed = partial[d, :, D + 2 * LANES :].astype(F32)
        terms = sum(pltpu.roll(packed, LANES - at, 1) for at in STATS_AT)
        stats.append(jnp.where(lane_ids(COLS) < 2 * HEADS, terms, 0.0))
    stats.append(fresh_stats[...])
    top = stats[0]
    for s in stats[1:]:
        top = jnp.maximum(top, s)
    scale = [jnp.exp(s - top) for s in stats]
    sums = [pltpu.roll(s, LANES - HEADS, 1) for s in stats]
    parts = [scale[d] * sums[d] for d in range(GROUP)]
    whole = scale[GROUP] * sums[GROUP]
    for p in parts:
        whole = whole + p
    weights = [p / whole for p in parts] + [scale[GROUP] / whole]
    low = lane_ids(COLS) < HEAD_DIM
    mixed = []
    for pair in range(PAIRS):
        at = slice(pair * LANES, (pair + 1) * LANES)
        sum_pair = jnp.zeros((COLS, LANES), F32)
        for d in range(GROUP + 1):
            w = jnp.where(
                low, weights[d][:, 2 * pair : 2 * pair + 1], weights[d][:, 2 * pair + 1 : 2 * pair + 2]
            )
            sum_pair += w * (partial[d, :, at].astype(F32) if d < GROUP else fresh[:, at])
        mixed.append(sum_pair.astype(BF16))
    attended[...] = dot(jnp.concatenate(mixed, axis=1), wo[...]).astype(BF16)


ANY_SPEC = pl.BlockSpec(memory_space=pl.ANY)
HBM_SPEC = pl.BlockSpec(memory_space=pltpu.HBM)


def params():
    return pltpu.CompilerParams(vmem_limit_bytes=VMEM)


def shape(dims, dtype=BF16):
    return jax.ShapeDtypeStruct(dims, dtype)


def local(block_input, stale_input, query_weight, key_weight, value_weight, out_weight, conv_weight):
    block = block_input.reshape(COLS, D)
    stale = stale_input.reshape(COLS, D)
    with jax.named_scope("payload"):
        payload = pl.pallas_call(
            payload_kernel,
            out_shape=shape((COLS + 16, D)),
            in_specs=[HBM_SPEC] * 2,
            scratch_shapes=[
                pltpu.VMEM((COLS, D), BF16),
                pltpu.VMEM((9, OWN, CO), BF16),
                pltpu.VMEM((16, D), F32),
                pltpu.SemaphoreType.DMA((2,)),
            ],
            compiler_params=params(),
        )(stale, conv_weight)
    gathered = lax.all_gather(payload, "z", axis=0)
    with jax.named_scope("prepare"):
        send, query = pl.pallas_call(
            prepare_kernel,
            out_shape=(shape((GROUP, COLS, SEND)), shape((COLS, D))),
            compiler_params=params(),
        )(block, gathered, query_weight, jnp.asarray(slice_matrix()))
    sent = lax.all_to_all(send, ("yh", "x"), 0, 0, tiled=True)
    other = lax.ppermute(gathered[:, COLS:, :], "core", [(0, 1), (1, 0)])
    with jax.named_scope("project"):
        keys, values = pl.pallas_call(
            project_kernel,
            out_shape=(shape((KEYS, D)), shape((KEYS, D))),
            in_specs=[pl.BlockSpec(memory_space=pltpu.VMEM)] * 3 + [ANY_SPEC],
            compiler_params=params(),
        )(gathered, key_weight, value_weight, send)
    with jax.named_scope("attend"):
        back = pl.pallas_call(
            attend_kernel,
            out_shape=shape((GROUP, COLS, BACK)),
            compiler_params=params(),
        )(sent, keys, values, gathered, other, jnp.asarray(tap_matrix()))
    partial = lax.all_to_all(back, ("yh", "x"), 0, 0, tiled=True)
    with jax.named_scope("fresh"):
        fresh, fresh_stats = pl.pallas_call(
            fresh_kernel,
            out_shape=(shape((COLS, D), F32), shape((COLS, LANES), F32)),
            in_specs=[pl.BlockSpec(memory_space=pltpu.VMEM)] * 4 + [ANY_SPEC],
            compiler_params=params(),
        )(block, query, key_weight, value_weight, back)
    with jax.named_scope("finish"):
        attended, convolved = pl.pallas_call(
            finish_kernel,
            out_shape=(shape((COLS, D)), shape((COLS, CO))),
            compiler_params=params(),
        )(partial, fresh, fresh_stats, out_weight)
    return attended.reshape(1, COLS, D), convolved.reshape(1, COLS, CO)


def solution(mesh):
    axes = Mesh(mesh.devices.reshape(Z, 2, 4, 2, 2), ("z", "yh", "x", "yl", "core"))
    rows, batch = ("z", "yh", "x"), ("yl", "core")
    placed = P(rows, batch, None)
    return jax.shard_map(
        local,
        mesh=axes,
        in_specs=(placed, placed, P(), P(), P(), P(), P(None, rows, None)),
        out_specs=(placed, placed),
        check_vma=False,
    )
```

```python
import jax
import jax.numpy as jnp
import ml_dtypes
import numpy as np
from jax import lax
from jax.experimental import pallas as pl
from jax.experimental.pallas import tpu as pltpu
from jax.sharding import Mesh, PartitionSpec as P

HEADS = 10
HEAD_DIM = 64
D = 640
CO = 320
COLS = 32
Z = 16
GROUP = 8
OWN = 5
LANES = 128
PAIRS = HEADS // 2
QUERIES = GROUP * COLS
KEYS = Z * COLS
SEND = D + 3 * LANES
BACK = D + 3 * LANES
STATS_AT = (64, 84, 104)
WIDE = 60
NARROW = 24
ATTEND = 52
F32 = jnp.float32
BF16 = jnp.bfloat16


def slice_matrix():
    out = np.zeros((D, GROUP * LANES), np.float32)
    for j in range(GROUP):
        for z in range(Z):
            for c in range(OWN):
                out[(z * GROUP + j) * OWN + c, LANES * j + 8 * z + c] = 1.0
    return out.astype(ml_dtypes.bfloat16)


def tap_matrix():
    row = lax.broadcasted_iota(jnp.int32, (3 * LANES, 2 * LANES), 0)
    col = lax.broadcasted_iota(jnp.int32, (3 * LANES, 2 * LANES), 1)
    z, c = (row % LANES) // 8, row % 8
    target = 16 * z + OWN * (row // LANES) + c
    return jnp.where((c < OWN) & (col == target), 1.0, 0.0).astype(BF16)


def layer_norm(values_in):
    mean = jnp.mean(values_in, axis=-1, keepdims=True)
    centered = values_in - mean
    variance = jnp.mean(centered * centered, axis=-1, keepdims=True)
    return (centered * lax.rsqrt(variance + 1e-05)).astype(BF16)


def silu(values_in):
    return (values_in * jax.nn.sigmoid(values_in)).astype(BF16)


def dot(a, b):
    return jnp.dot(a, b, preferred_element_type=F32)


def dot_t(a, b):
    return lax.dot_general(a, b, (((1,), (1,)), ((), ())), preferred_element_type=F32)


def lane_ids(rows):
    return lax.broadcasted_iota(jnp.int32, (rows, LANES), 1)


def place():
    return lax.axis_index("z"), lax.axis_index("yh") * 4 + lax.axis_index("x")


def payload_kernel(stale_hbm, taps_hbm, gather, stale, taps, rows, sems):
    copies = [
        pltpu.make_async_copy(taps_hbm, taps, sems.at[0]),
        pltpu.make_async_copy(stale_hbm, stale, sems.at[1]),
    ]
    for copy in copies:
        copy.start()
    core = lax.axis_index("core")
    rows[...] = jnp.zeros_like(rows)
    copies[0].wait()
    for dx in range(3):
        first = jnp.where(core == 0, taps[dx].astype(F32), taps[6 + dx].astype(F32))
        second = jnp.where(core == 0, taps[3 + dx].astype(F32), 0.0)
        rows[OWN * dx : OWN * (dx + 1), :] = jnp.concatenate([first, second], axis=1)
    gather[COLS:, :] = rows[...].astype(BF16)
    copies[1].wait()
    gather[:COLS, :] = stale[...]


def prepare_kernel(block, stale, gathered, wq, slices, send, query_out, halo_rows, sem):
    z, j = place()
    beside = jnp.where(j == 0, jnp.minimum(z + 1, Z - 1), jnp.maximum(z - 1, 0))
    fetch = pltpu.make_async_copy(gathered.at[beside, pl.ds(0, COLS), :], halo_rows, sem)
    fetch.start()
    query = dot(layer_norm(block[...].astype(F32)), wq[...]).astype(BF16)
    query = query * jnp.array(HEAD_DIM**-0.5, BF16)
    query_out[...] = query
    outside = ((j == 0) & (z == Z - 1)) | ((j != 0) & (z == 0))
    fetch.wait()
    halo = halo_rows[...].astype(F32) * jnp.where(outside, 0.0, 1.0)
    three = jnp.concatenate(
        [silu(block[...].astype(F32)), silu(stale[...].astype(F32)), silu(halo)], axis=0
    )
    cut = dot(three, slices[...]).astype(BF16)
    for j in range(GROUP):
        send[j, :, :D] = query
        for part in range(3):
            send[j, :, D + part * LANES : D + (part + 1) * LANES] = cut[
                part * COLS : (part + 1) * COLS, j * LANES : (j + 1) * LANES
            ]


def project_kernel(gathered, wk, wv, after, both):
    del after
    normed = layer_norm(gathered[:, :COLS, :].reshape(KEYS, D).astype(F32))
    both[:, :D] = dot(normed, wk[...]).astype(BF16)
    both[:, D:] = dot(normed, wv[...]).astype(BF16)


def attend_pair(query, keys, values, masked, lanes):
    low = lanes < HEAD_DIM
    zero = jnp.zeros_like(query)
    two = jnp.concatenate([jnp.where(low, query, zero), jnp.where(low, zero, query)], axis=0)
    scores = dot_t(two, keys)
    if masked is not None:
        scores = jnp.where(masked, -1e30, scores)
    row_max = jnp.max(scores, axis=-1, keepdims=True)
    exp_scores = jnp.exp(scores - row_max)
    row_sum = jnp.sum(exp_scores, axis=-1, keepdims=True)
    weighted = dot(exp_scores.astype(BF16), values)
    return row_max, row_sum, weighted


def convolve(sent, gathered, other):
    spread = tap_matrix()
    mine = gathered[:, COLS:, :].reshape(Z * 16, D)
    theirs = other[...].reshape(Z * 16, D)
    zero_core = lax.axis_index("core") == 0
    lower_half = jnp.where(zero_core, mine, theirs)
    upper_half = jnp.where(zero_core, theirs, mine)
    weights = (lower_half[:, :CO], lower_half[:, CO:], upper_half[:, :CO])
    active = sent[:, :, D : D + LANES]
    stale = sent[:, :, D + LANES : D + 2 * LANES]
    upper = jnp.concatenate([sent[7:8, :, D + 2 * LANES :], stale[:7]], axis=0)
    lower = jnp.concatenate([stale[1:], sent[0:1, :, D + 2 * LANES :]], axis=0)
    column = lax.broadcasted_iota(jnp.int32, (QUERIES, LANES), 0) % COLS
    total = jnp.zeros((QUERIES, CO), F32)
    for dy, source in enumerate((upper, active, lower)):
        rows = source.reshape(QUERIES, LANES).astype(F32)
        left = jnp.where(column == 0, 0.0, pltpu.roll(rows, 1, 0))
        right = jnp.where(column == COLS - 1, 0.0, pltpu.roll(rows, QUERIES - 1, 0))
        three = jnp.concatenate([left.astype(BF16), rows.astype(BF16), right.astype(BF16)], axis=1)
        total += dot(dot(three, spread).astype(BF16), weights[dy])
    return total


def attend_kernel(sent, both, gathered, other, back):
    z, j = place()
    row = lax.broadcasted_iota(jnp.int32, (2 * QUERIES, KEYS), 0)
    col = lax.broadcasted_iota(jnp.int32, (2 * QUERIES, KEYS), 1)
    masked = (((row // COLS) % GROUP) == j) & ((col // COLS) == z)
    lanes = lane_ids(QUERIES)
    low = lanes < HEAD_DIM
    stats = jnp.zeros((QUERIES, LANES), F32)
    for pair in range(PAIRS):
        at = slice(pair * LANES, (pair + 1) * LANES)
        query = sent[:, :, at].reshape(QUERIES, LANES)
        keys, values = both[:, at], both[:, D + pair * LANES : D + (pair + 1) * LANES]
        row_max, row_sum, weighted = attend_pair(query, keys, values, masked, lanes)
        weighted = weighted / row_sum
        mixed = jnp.where(low, weighted[:QUERIES], weighted[QUERIES:])
        back[:, :, at] = mixed.astype(BF16).reshape(GROUP, COLS, LANES)
        for half in range(2):
            head = 2 * pair + half
            at_rows = slice(half * QUERIES, (half + 1) * QUERIES)
            stats = jnp.where(lanes == head, row_max[at_rows], stats)
            stats = jnp.where(lanes == HEADS + head, row_sum[at_rows], stats)
    high = stats.astype(BF16).astype(F32)
    rest = stats - high
    middle = rest.astype(BF16).astype(F32)
    last = rest - middle
    packed = sum(pltpu.roll(term, at, 1) for term, at in zip((high, middle, last), STATS_AT))
    total = convolve(sent, gathered, other)
    back[:, :, D : D + 2 * LANES] = (
        total[:, : 2 * LANES].astype(BF16).reshape(GROUP, COLS, 2 * LANES)
    )
    tail = jnp.concatenate([total[:, 2 * LANES :], packed[:, CO - 2 * LANES :]], axis=1)
    back[:, :, D + 2 * LANES :] = tail.astype(BF16).reshape(GROUP, COLS, LANES)


def fresh_kernel(block, query, wk, wv, after, weighted_out, stats_out):
    del after
    normed = layer_norm(block[...].astype(F32))
    keys = dot(normed, wk[...]).astype(BF16)
    values = dot(normed, wv[...]).astype(BF16)
    lanes = lane_ids(COLS)
    low = lanes < HEAD_DIM
    stats = jnp.zeros((COLS, LANES), F32)
    for pair in range(PAIRS):
        at = slice(pair * LANES, (pair + 1) * LANES)
        row_max, row_sum, weighted = attend_pair(
            query[:, at], keys[:, at], values[:, at], None, lanes
        )
        weighted_out[:, at] = jnp.where(low, weighted[:COLS], weighted[COLS:])
        for half in range(2):
            head = 2 * pair + half
            at_rows = slice(half * COLS, (half + 1) * COLS)
            stats = jnp.where(lanes == head, row_max[at_rows], stats)
            stats = jnp.where(lanes == HEADS + head, row_sum[at_rows], stats)
    stats_out[...] = stats


def finish_kernel(partial, fresh, fresh_stats, wo, attended, convolved):
    total = jnp.zeros((COLS, CO), F32)
    for d in range(GROUP):
        total += partial[d, :, D : D + CO].astype(F32)
    convolved[...] = total.astype(BF16)
    stats = []
    for d in range(GROUP):
        packed = partial[d, :, D + 2 * LANES :].astype(F32)
        terms = sum(pltpu.roll(packed, LANES - at, 1) for at in STATS_AT)
        stats.append(jnp.where(lane_ids(COLS) < 2 * HEADS, terms, 0.0))
    stats.append(fresh_stats[...])
    top = stats[0]
    for s in stats[1:]:
        top = jnp.maximum(top, s)
    scale = [jnp.exp(s - top) for s in stats]
    sums = [pltpu.roll(s, LANES - HEADS, 1) for s in stats]
    parts = [scale[d] * sums[d] for d in range(GROUP)]
    whole = scale[GROUP] * sums[GROUP]
    for p in parts:
        whole = whole + p
    weights = [p / whole for p in parts] + [scale[GROUP] / whole]
    low = lane_ids(COLS) < HEAD_DIM
    mixed = []
    for pair in range(PAIRS):
        at = slice(pair * LANES, (pair + 1) * LANES)
        sum_pair = jnp.zeros((COLS, LANES), F32)
        for d in range(GROUP + 1):
            w = jnp.where(
                low, weights[d][:, 2 * pair : 2 * pair + 1], weights[d][:, 2 * pair + 1 : 2 * pair + 2]
            )
            sum_pair += w * (partial[d, :, at].astype(F32) if d < GROUP else fresh[:, at])
        mixed.append(sum_pair.astype(BF16))
    attended[...] = dot(jnp.concatenate(mixed, axis=1), wo[...]).astype(BF16)


ANY_SPEC = pl.BlockSpec(memory_space=pl.ANY)
VMEM_SPEC = pl.BlockSpec(memory_space=pltpu.VMEM)
HBM_SPEC = pl.BlockSpec(memory_space=pltpu.HBM)


def params(mib):
    return pltpu.CompilerParams(vmem_limit_bytes=mib * 1024 * 1024)


def shape(dims, dtype=BF16):
    return jax.ShapeDtypeStruct(dims, dtype)


def local(block_input, stale_input, query_weight, key_weight, value_weight, out_weight, conv_weight):
    block = block_input.reshape(COLS, D)
    stale = stale_input.reshape(COLS, D)
    with jax.named_scope("payload"):
        payload = pl.pallas_call(
            payload_kernel,
            out_shape=shape((COLS + 16, D)),
            in_specs=[HBM_SPEC] * 2,
            scratch_shapes=[
                pltpu.VMEM((COLS, D), BF16),
                pltpu.VMEM((9, OWN, CO), BF16),
                pltpu.VMEM((16, D), F32),
                pltpu.SemaphoreType.DMA((2,)),
            ],
            compiler_params=params(WIDE),
        )(stale, conv_weight)
    gathered = lax.all_gather(payload, "z", axis=0)
    with jax.named_scope("prepare"):
        send, query = pl.pallas_call(
            prepare_kernel,
            out_shape=(shape((GROUP, COLS, SEND)), shape((COLS, D))),
            in_specs=[VMEM_SPEC, VMEM_SPEC, HBM_SPEC, VMEM_SPEC, VMEM_SPEC],
            scratch_shapes=[pltpu.VMEM((COLS, D), BF16), pltpu.SemaphoreType.DMA],
            compiler_params=params(WIDE),
        )(block, stale, gathered, query_weight, jnp.asarray(slice_matrix()))
    sent = lax.all_to_all(send, ("yh", "x"), 0, 0, tiled=True)
    other = lax.ppermute(gathered[:, COLS:, :], "core", [(0, 1), (1, 0)])
    with jax.named_scope("project"):
        both = pl.pallas_call(
            project_kernel,
            out_shape=shape((KEYS, 2 * D)),
            in_specs=[VMEM_SPEC] * 3 + [ANY_SPEC],
            compiler_params=params(WIDE),
        )(gathered, key_weight, value_weight, send)
    with jax.named_scope("attend"):
        back = pl.pallas_call(
            attend_kernel,
            out_shape=shape((GROUP, COLS, BACK)),
            compiler_params=params(ATTEND),
        )(sent, both, gathered, other)
    partial = lax.all_to_all(back, ("yh", "x"), 0, 0, tiled=True)
    with jax.named_scope("fresh"):
        fresh, fresh_stats = pl.pallas_call(
            fresh_kernel,
            out_shape=(shape((COLS, D), F32), shape((COLS, LANES), F32)),
            in_specs=[VMEM_SPEC] * 4 + [ANY_SPEC],
            compiler_params=params(NARROW),
        )(block, query, key_weight, value_weight, back)
    with jax.named_scope("finish"):
        attended, convolved = pl.pallas_call(
            finish_kernel,
            out_shape=(shape((COLS, D)), shape((COLS, CO))),
            compiler_params=params(NARROW),
        )(partial, fresh, fresh_stats, out_weight)
    return attended.reshape(1, COLS, D), convolved.reshape(1, COLS, CO)


def solution(mesh):
    axes = Mesh(mesh.devices.reshape(Z, 2, 4, 2, 2), ("z", "yh", "x", "yl", "core"))
    rows, batch = ("z", "yh", "x"), ("yl", "core")
    placed = P(rows, batch, None)
    return jax.shard_map(
        local,
        mesh=axes,
        in_specs=(placed, placed, P(), P(), P(), P(), P(None, rows, None)),
        out_specs=(placed, placed),
        check_vma=False,
    )
```

```python
import jax
import jax.numpy as jnp
import ml_dtypes
import numpy as np
from jax import lax
from jax.experimental import pallas as pl
from jax.experimental.pallas import tpu as pltpu
from jax.sharding import Mesh, PartitionSpec as P

HEADS = 10
HEAD_DIM = 64
D = 640
CO = 320
COLS = 32
Z = 16
GROUP = 8
OWN = 5
LANES = 128
PAIRS = HEADS // 2
QUERIES = GROUP * COLS
KEYS = Z * COLS
SEND = D + 3 * LANES
BACK = D + 3 * LANES
VMEM = 24 * 1024 * 1024
PAYLOAD, PREPARE, PROJECT, ATTEND, FRESH, FINISH = 1, 2, 2, 3, 1, 2
STATS_AT = (64, 84, 104)
F32 = jnp.float32
BF16 = jnp.bfloat16


def slice_matrix():
    out = np.zeros((D, GROUP * LANES), np.float32)
    for j in range(GROUP):
        for z in range(Z):
            for c in range(OWN):
                out[(z * GROUP + j) * OWN + c, LANES * j + 8 * z + c] = 1.0
    return out.astype(ml_dtypes.bfloat16)


def tap_matrix():
    row = lax.broadcasted_iota(jnp.int32, (3 * LANES, 2 * LANES), 0)
    col = lax.broadcasted_iota(jnp.int32, (3 * LANES, 2 * LANES), 1)
    z, c = (row % LANES) // 8, row % 8
    target = 16 * z + OWN * (row // LANES) + c
    return jnp.where((c < OWN) & (col == target), 1.0, 0.0).astype(BF16)


def layer_norm(values_in):
    mean = jnp.mean(values_in, axis=-1, keepdims=True)
    centered = values_in - mean
    variance = jnp.mean(centered * centered, axis=-1, keepdims=True)
    return (centered * lax.rsqrt(variance + 1e-05)).astype(BF16)


def silu(values_in):
    return (values_in * jax.nn.sigmoid(values_in)).astype(BF16)


def dot(a, b):
    return jnp.dot(a, b, preferred_element_type=F32)


def dot_t(a, b):
    return lax.dot_general(a, b, (((1,), (1,)), ((), ())), preferred_element_type=F32)


def lane_ids(rows):
    return lax.broadcasted_iota(jnp.int32, (rows, LANES), 1)


def place():
    return lax.axis_index("z"), lax.axis_index("yh") * 4 + lax.axis_index("x")


def payload_kernel(stale_hbm, taps_hbm, gather, stale, taps, rows, sems):
    copies = [
        pltpu.make_async_copy(taps_hbm, taps, sems.at[0]),
        pltpu.make_async_copy(stale_hbm, stale, sems.at[1]),
    ]
    for copy in copies:
        copy.start()
    core = lax.axis_index("core")
    rows[...] = jnp.zeros_like(rows)
    copies[0].wait()
    for dx in range(3):
        first = jnp.where(core == 0, taps[dx].astype(F32), taps[6 + dx].astype(F32))
        second = jnp.where(core == 0, taps[3 + dx].astype(F32), 0.0)
        rows[OWN * dx : OWN * (dx + 1), :] = jnp.concatenate([first, second], axis=1)
    gather[COLS:, :] = rows[...].astype(BF16)
    copies[1].wait()
    gather[:COLS, :] = stale[...]


def prepare_kernel(block, gathered, wq, slices, send, query_out):
    z, j = place()
    beside = jnp.where(j == 0, jnp.minimum(z + 1, Z - 1), jnp.maximum(z - 1, 0))
    stale = gathered[z, :COLS, :]
    query = dot(layer_norm(block[...].astype(F32)), wq[...]).astype(BF16)
    query = query * jnp.array(HEAD_DIM**-0.5, BF16)
    query_out[...] = query
    outside = ((j == 0) & (z == Z - 1)) | ((j != 0) & (z == 0))
    halo = gathered[beside, :COLS, :].astype(F32) * jnp.where(outside, 0.0, 1.0)
    three = jnp.concatenate(
        [silu(block[...].astype(F32)), silu(stale.astype(F32)), silu(halo)], axis=0
    )
    cut = dot(three, slices[...]).astype(BF16)
    for j in range(GROUP):
        send[j, :, :D] = query
        for part in range(3):
            send[j, :, D + part * LANES : D + (part + 1) * LANES] = cut[
                part * COLS : (part + 1) * COLS, j * LANES : (j + 1) * LANES
            ]


def project_kernel(gathered, wk, wv, after, both):
    del after
    normed = layer_norm(gathered[:, :COLS, :].reshape(KEYS, D).astype(F32))
    both[:, :D] = dot(normed, wk[...]).astype(BF16)
    both[:, D:] = dot(normed, wv[...]).astype(BF16)


def attend_pair(query, keys, values, masked, lanes):
    low = lanes < HEAD_DIM
    zero = jnp.zeros_like(query)
    two = jnp.concatenate([jnp.where(low, query, zero), jnp.where(low, zero, query)], axis=0)
    scores = dot_t(two, keys)
    if masked is not None:
        scores = jnp.where(masked, -1e30, scores)
    row_max = jnp.max(scores, axis=-1, keepdims=True)
    exp_scores = jnp.exp(scores - row_max)
    row_sum = jnp.sum(exp_scores, axis=-1, keepdims=True)
    weighted = dot(exp_scores.astype(BF16), values)
    return row_max, row_sum, weighted


def convolve(sent, gathered, other):
    spread = tap_matrix()
    mine = gathered[:, COLS:, :].reshape(Z * 16, D)
    theirs = other[...].reshape(Z * 16, D)
    zero_core = lax.axis_index("core") == 0
    lower_half = jnp.where(zero_core, mine, theirs)
    upper_half = jnp.where(zero_core, theirs, mine)
    weights = (lower_half[:, :CO], lower_half[:, CO:], upper_half[:, :CO])
    active = sent[:, :, D : D + LANES]
    stale = sent[:, :, D + LANES : D + 2 * LANES]
    upper = jnp.concatenate([sent[7:8, :, D + 2 * LANES :], stale[:7]], axis=0)
    lower = jnp.concatenate([stale[1:], sent[0:1, :, D + 2 * LANES :]], axis=0)
    column = lax.broadcasted_iota(jnp.int32, (QUERIES, LANES), 0) % COLS
    total = jnp.zeros((QUERIES, CO), F32)
    for dy, source in enumerate((upper, active, lower)):
        rows = source.reshape(QUERIES, LANES).astype(F32)
        left = jnp.where(column == 0, 0.0, pltpu.roll(rows, 1, 0))
        right = jnp.where(column == COLS - 1, 0.0, pltpu.roll(rows, QUERIES - 1, 0))
        three = jnp.concatenate([left.astype(BF16), rows.astype(BF16), right.astype(BF16)], axis=1)
        total += dot(dot(three, spread).astype(BF16), weights[dy])
    return total


def attend_kernel(sent, both, gathered, other, back):
    z, j = place()
    row = lax.broadcasted_iota(jnp.int32, (2 * QUERIES, KEYS), 0)
    col = lax.broadcasted_iota(jnp.int32, (2 * QUERIES, KEYS), 1)
    masked = (((row // COLS) % GROUP) == j) & ((col // COLS) == z)
    lanes = lane_ids(QUERIES)
    low = lanes < HEAD_DIM
    stats = jnp.zeros((QUERIES, LANES), F32)
    for pair in range(PAIRS):
        at = slice(pair * LANES, (pair + 1) * LANES)
        query = sent[:, :, at].reshape(QUERIES, LANES)
        keys, values = both[:, at], both[:, D + pair * LANES : D + (pair + 1) * LANES]
        row_max, row_sum, weighted = attend_pair(query, keys, values, masked, lanes)
        weighted = weighted / row_sum
        mixed = jnp.where(low, weighted[:QUERIES], weighted[QUERIES:])
        back[:, :, at] = mixed.astype(BF16).reshape(GROUP, COLS, LANES)
        for half in range(2):
            head = 2 * pair + half
            at_rows = slice(half * QUERIES, (half + 1) * QUERIES)
            stats = jnp.where(lanes == head, row_max[at_rows], stats)
            stats = jnp.where(lanes == HEADS + head, row_sum[at_rows], stats)
    high = stats.astype(BF16).astype(F32)
    rest = stats - high
    middle = rest.astype(BF16).astype(F32)
    last = rest - middle
    packed = sum(pltpu.roll(term, at, 1) for term, at in zip((high, middle, last), STATS_AT))
    total = convolve(sent, gathered, other)
    back[:, :, D : D + 2 * LANES] = (
        total[:, : 2 * LANES].astype(BF16).reshape(GROUP, COLS, 2 * LANES)
    )
    tail = jnp.concatenate([total[:, 2 * LANES :], packed[:, CO - 2 * LANES :]], axis=1)
    back[:, :, D + 2 * LANES :] = tail.astype(BF16).reshape(GROUP, COLS, LANES)


def fresh_kernel(block, query, wk, wv, after, weighted_out, stats_out):
    del after
    normed = layer_norm(block[...].astype(F32))
    keys = dot(normed, wk[...]).astype(BF16)
    values = dot(normed, wv[...]).astype(BF16)
    lanes = lane_ids(COLS)
    low = lanes < HEAD_DIM
    stats = jnp.zeros((COLS, LANES), F32)
    for pair in range(PAIRS):
        at = slice(pair * LANES, (pair + 1) * LANES)
        row_max, row_sum, weighted = attend_pair(
            query[:, at], keys[:, at], values[:, at], None, lanes
        )
        weighted_out[:, at] = jnp.where(low, weighted[:COLS], weighted[COLS:])
        for half in range(2):
            head = 2 * pair + half
            at_rows = slice(half * COLS, (half + 1) * COLS)
            stats = jnp.where(lanes == head, row_max[at_rows], stats)
            stats = jnp.where(lanes == HEADS + head, row_sum[at_rows], stats)
    stats_out[...] = stats


def finish_kernel(partial, fresh, fresh_stats, wo, attended, convolved):
    total = jnp.zeros((COLS, CO), F32)
    for d in range(GROUP):
        total += partial[d, :, D : D + CO].astype(F32)
    convolved[...] = total.astype(BF16)
    stats = []
    for d in range(GROUP):
        packed = partial[d, :, D + 2 * LANES :].astype(F32)
        terms = sum(pltpu.roll(packed, LANES - at, 1) for at in STATS_AT)
        stats.append(jnp.where(lane_ids(COLS) < 2 * HEADS, terms, 0.0))
    stats.append(fresh_stats[...])
    top = stats[0]
    for s in stats[1:]:
        top = jnp.maximum(top, s)
    scale = [jnp.exp(s - top) for s in stats]
    sums = [pltpu.roll(s, LANES - HEADS, 1) for s in stats]
    parts = [scale[d] * sums[d] for d in range(GROUP)]
    whole = scale[GROUP] * sums[GROUP]
    for p in parts:
        whole = whole + p
    weights = [p / whole for p in parts] + [scale[GROUP] / whole]
    low = lane_ids(COLS) < HEAD_DIM
    mixed = []
    for pair in range(PAIRS):
        at = slice(pair * LANES, (pair + 1) * LANES)
        sum_pair = jnp.zeros((COLS, LANES), F32)
        for d in range(GROUP + 1):
            w = jnp.where(
                low, weights[d][:, 2 * pair : 2 * pair + 1], weights[d][:, 2 * pair + 1 : 2 * pair + 2]
            )
            sum_pair += w * (partial[d, :, at].astype(F32) if d < GROUP else fresh[:, at])
        mixed.append(sum_pair.astype(BF16))
    attended[...] = dot(jnp.concatenate(mixed, axis=1), wo[...]).astype(BF16)


ANY_SPEC = pl.BlockSpec(memory_space=pl.ANY)
VMEM_SPEC = pl.BlockSpec(memory_space=pltpu.VMEM)
HBM_SPEC = pl.BlockSpec(memory_space=pltpu.HBM)


def params():
    return pltpu.CompilerParams(vmem_limit_bytes=VMEM)


def cost(us):
    return pl.CostEstimate(flops=int(us * 1e9), bytes_accessed=0, transcendentals=0)


def shape(dims, dtype=BF16):
    return jax.ShapeDtypeStruct(dims, dtype)


def local(block_input, stale_input, query_weight, key_weight, value_weight, out_weight, conv_weight):
    block = block_input.reshape(COLS, D)
    stale = stale_input.reshape(COLS, D)
    with jax.named_scope("payload"):
        payload = pl.pallas_call(
            payload_kernel,
            out_shape=shape((COLS + 16, D)),
            in_specs=[HBM_SPEC] * 2,
            scratch_shapes=[
                pltpu.VMEM((COLS, D), BF16),
                pltpu.VMEM((9, OWN, CO), BF16),
                pltpu.VMEM((16, D), F32),
                pltpu.SemaphoreType.DMA((2,)),
            ],
            compiler_params=params(),
            cost_estimate=cost(PAYLOAD),
        )(stale, conv_weight)
    gathered = lax.all_gather(payload, "z", axis=0)
    with jax.named_scope("prepare"):
        send, query = pl.pallas_call(
            prepare_kernel,
            out_shape=(shape((GROUP, COLS, SEND)), shape((COLS, D))),
            compiler_params=params(),
            cost_estimate=cost(PREPARE),
        )(block, gathered, query_weight, jnp.asarray(slice_matrix()))
    sent = lax.all_to_all(send, ("yh", "x"), 0, 0, tiled=True)
    other = lax.ppermute(gathered[:, COLS:, :], "core", [(0, 1), (1, 0)])
    with jax.named_scope("project"):
        both = pl.pallas_call(
            project_kernel,
            out_shape=shape((KEYS, 2 * D)),
            in_specs=[VMEM_SPEC] * 3 + [ANY_SPEC],
            compiler_params=params(),
            cost_estimate=cost(PROJECT),
        )(gathered, key_weight, value_weight, send)
    with jax.named_scope("attend"):
        back = pl.pallas_call(
            attend_kernel,
            out_shape=shape((GROUP, COLS, BACK)),
            compiler_params=params(),
            cost_estimate=cost(ATTEND),
        )(sent, both, gathered, other)
    partial = lax.all_to_all(back, ("yh", "x"), 0, 0, tiled=True)
    with jax.named_scope("fresh"):
        fresh, fresh_stats = pl.pallas_call(
            fresh_kernel,
            out_shape=(shape((COLS, D), F32), shape((COLS, LANES), F32)),
            in_specs=[VMEM_SPEC] * 4 + [ANY_SPEC],
            compiler_params=params(),
            cost_estimate=cost(FRESH),
        )(block, query, key_weight, value_weight, back)
    with jax.named_scope("finish"):
        attended, convolved = pl.pallas_call(
            finish_kernel,
            out_shape=(shape((COLS, D)), shape((COLS, CO))),
            compiler_params=params(),
            cost_estimate=cost(FINISH),
        )(partial, fresh, fresh_stats, out_weight)
    return attended.reshape(1, COLS, D), convolved.reshape(1, COLS, CO)


def solution(mesh):
    axes = Mesh(mesh.devices.reshape(Z, 2, 4, 2, 2), ("z", "yh", "x", "yl", "core"))
    rows, batch = ("z", "yh", "x"), ("yl", "core")
    placed = P(rows, batch, None)
    return jax.shard_map(
        local,
        mesh=axes,
        in_specs=(placed, placed, P(), P(), P(), P(), P(None, rows, None)),
        out_specs=(placed, placed),
        check_vma=False,
    )
```

```python
import jax
import jax.numpy as jnp
import ml_dtypes
import numpy as np
from jax import lax
from jax.experimental import pallas as pl
from jax.experimental.pallas import tpu as pltpu
from jax.sharding import Mesh, PartitionSpec as P

HEADS = 10
HEAD_DIM = 64
D = 640
CO = 320
COLS = 32
Z = 16
GROUP = 8
OWN = 5
LANES = 128
PAIRS = HEADS // 2
QUERIES = GROUP * COLS
KEYS = Z * COLS
SEND = D + 3 * LANES
BACK = D + 3 * LANES
VMEM = 24 * 1024 * 1024
PAYLOAD, PREPARE, PROJECT, ATTEND, FRESH, FINISH = 1, 2, 2, 3, 1, 2
STATS_AT = (64, 84, 104)
F32 = jnp.float32
BF16 = jnp.bfloat16


def slice_matrix():
    out = np.zeros((D, GROUP * LANES), np.float32)
    for j in range(GROUP):
        for z in range(Z):
            for c in range(OWN):
                out[(z * GROUP + j) * OWN + c, LANES * j + 8 * z + c] = 1.0
    return out.astype(ml_dtypes.bfloat16)


def tap_matrix():
    row = lax.broadcasted_iota(jnp.int32, (3 * LANES, 2 * LANES), 0)
    col = lax.broadcasted_iota(jnp.int32, (3 * LANES, 2 * LANES), 1)
    z, c = (row % LANES) // 8, row % 8
    target = 16 * z + OWN * (row // LANES) + c
    return jnp.where((c < OWN) & (col == target), 1.0, 0.0).astype(BF16)


def layer_norm(values_in):
    mean = jnp.mean(values_in, axis=-1, keepdims=True)
    centered = values_in - mean
    variance = jnp.mean(centered * centered, axis=-1, keepdims=True)
    return (centered * lax.rsqrt(variance + 1e-05)).astype(BF16)


def silu(values_in):
    return (values_in * jax.nn.sigmoid(values_in)).astype(BF16)


def dot(a, b):
    return jnp.dot(a, b, preferred_element_type=F32)


def dot_t(a, b):
    return lax.dot_general(a, b, (((1,), (1,)), ((), ())), preferred_element_type=F32)


def lane_ids(rows):
    return lax.broadcasted_iota(jnp.int32, (rows, LANES), 1)


def place():
    return lax.axis_index("z"), lax.axis_index("yh") * 4 + lax.axis_index("x")


def payload_kernel(stale_hbm, taps_hbm, gather, stale, taps, rows, sems):
    copies = [
        pltpu.make_async_copy(taps_hbm, taps, sems.at[0]),
        pltpu.make_async_copy(stale_hbm, stale, sems.at[1]),
    ]
    for copy in copies:
        copy.start()
    core = lax.axis_index("core")
    rows[...] = jnp.zeros_like(rows)
    copies[0].wait()
    for dx in range(3):
        first = jnp.where(core == 0, taps[dx].astype(F32), taps[6 + dx].astype(F32))
        second = jnp.where(core == 0, taps[3 + dx].astype(F32), 0.0)
        rows[OWN * dx : OWN * (dx + 1), :] = jnp.concatenate([first, second], axis=1)
    gather[COLS:, :] = rows[...].astype(BF16)
    copies[1].wait()
    gather[:COLS, :] = stale[...]


def prepare_kernel(block, gathered, wq, slices, send, query_out):
    z, j = place()
    beside = jnp.where(j == 0, jnp.minimum(z + 1, Z - 1), jnp.maximum(z - 1, 0))
    stale = gathered[z, :COLS, :]
    query = dot(layer_norm(block[...].astype(F32)), wq[...]).astype(BF16)
    query = query * jnp.array(HEAD_DIM**-0.5, BF16)
    query_out[...] = query
    outside = ((j == 0) & (z == Z - 1)) | ((j != 0) & (z == 0))
    halo = gathered[beside, :COLS, :].astype(F32) * jnp.where(outside, 0.0, 1.0)
    three = jnp.concatenate(
        [silu(block[...].astype(F32)), silu(stale.astype(F32)), silu(halo)], axis=0
    )
    cut = dot(three, slices[...]).astype(BF16)
    for j in range(GROUP):
        send[j, :, :D] = query
        for part in range(3):
            send[j, :, D + part * LANES : D + (part + 1) * LANES] = cut[
                part * COLS : (part + 1) * COLS, j * LANES : (j + 1) * LANES
            ]


def project_kernel(gathered, block, weight, after, out, own):
    del after
    normed = layer_norm(gathered[:, :COLS, :].reshape(KEYS, D).astype(F32))
    fresh = layer_norm(block[...].astype(F32))
    out[...] = dot(normed, weight[...]).astype(BF16)
    own[...] = dot(fresh, weight[...]).astype(BF16)


def attend_pair(query, keys, values, masked, lanes):
    low = lanes < HEAD_DIM
    zero = jnp.zeros_like(query)
    two = jnp.concatenate([jnp.where(low, query, zero), jnp.where(low, zero, query)], axis=0)
    scores = dot_t(two, keys)
    if masked is not None:
        scores = jnp.where(masked, -1e30, scores)
    row_max = jnp.max(scores, axis=-1, keepdims=True)
    exp_scores = jnp.exp(scores - row_max)
    row_sum = jnp.sum(exp_scores, axis=-1, keepdims=True)
    weighted = dot(exp_scores.astype(BF16), values)
    return row_max, row_sum, weighted


def convolve(sent, gathered, other):
    spread = tap_matrix()
    mine = gathered[:, COLS:, :].reshape(Z * 16, D)
    theirs = other[...].reshape(Z * 16, D)
    zero_core = lax.axis_index("core") == 0
    lower_half = jnp.where(zero_core, mine, theirs)
    upper_half = jnp.where(zero_core, theirs, mine)
    weights = (lower_half[:, :CO], lower_half[:, CO:], upper_half[:, :CO])
    active = sent[:, :, D : D + LANES]
    stale = sent[:, :, D + LANES : D + 2 * LANES]
    upper = jnp.concatenate([sent[7:8, :, D + 2 * LANES :], stale[:7]], axis=0)
    lower = jnp.concatenate([stale[1:], sent[0:1, :, D + 2 * LANES :]], axis=0)
    column = lax.broadcasted_iota(jnp.int32, (QUERIES, LANES), 0) % COLS
    total = jnp.zeros((QUERIES, CO), F32)
    for dy, source in enumerate((upper, active, lower)):
        rows = source.reshape(QUERIES, LANES).astype(F32)
        left = jnp.where(column == 0, 0.0, pltpu.roll(rows, 1, 0))
        right = jnp.where(column == COLS - 1, 0.0, pltpu.roll(rows, QUERIES - 1, 0))
        three = jnp.concatenate([left.astype(BF16), rows.astype(BF16), right.astype(BF16)], axis=1)
        total += dot(dot(three, spread).astype(BF16), weights[dy])
    return total


def attend_kernel(sent, all_keys, all_values, gathered, other, back):
    z, j = place()
    row = lax.broadcasted_iota(jnp.int32, (2 * QUERIES, KEYS), 0)
    col = lax.broadcasted_iota(jnp.int32, (2 * QUERIES, KEYS), 1)
    masked = (((row // COLS) % GROUP) == j) & ((col // COLS) == z)
    lanes = lane_ids(QUERIES)
    low = lanes < HEAD_DIM
    stats = jnp.zeros((QUERIES, LANES), F32)
    for pair in range(PAIRS):
        at = slice(pair * LANES, (pair + 1) * LANES)
        query = sent[:, :, at].reshape(QUERIES, LANES)
        keys, values = all_keys[:, at], all_values[:, at]
        row_max, row_sum, weighted = attend_pair(query, keys, values, masked, lanes)
        weighted = weighted / row_sum
        mixed = jnp.where(low, weighted[:QUERIES], weighted[QUERIES:])
        back[:, :, at] = mixed.astype(BF16).reshape(GROUP, COLS, LANES)
        for half in range(2):
            head = 2 * pair + half
            at_rows = slice(half * QUERIES, (half + 1) * QUERIES)
            stats = jnp.where(lanes == head, row_max[at_rows], stats)
            stats = jnp.where(lanes == HEADS + head, row_sum[at_rows], stats)
    high = stats.astype(BF16).astype(F32)
    rest = stats - high
    middle = rest.astype(BF16).astype(F32)
    last = rest - middle
    packed = sum(pltpu.roll(term, at, 1) for term, at in zip((high, middle, last), STATS_AT))
    total = convolve(sent, gathered, other)
    back[:, :, D : D + 2 * LANES] = (
        total[:, : 2 * LANES].astype(BF16).reshape(GROUP, COLS, 2 * LANES)
    )
    tail = jnp.concatenate([total[:, 2 * LANES :], packed[:, CO - 2 * LANES :]], axis=1)
    back[:, :, D + 2 * LANES :] = tail.astype(BF16).reshape(GROUP, COLS, LANES)


def fresh_kernel(own_keys, own_values, query, after, weighted_out, stats_out):
    del after
    lanes = lane_ids(COLS)
    low = lanes < HEAD_DIM
    stats = jnp.zeros((COLS, LANES), F32)
    for pair in range(PAIRS):
        at = slice(pair * LANES, (pair + 1) * LANES)
        row_max, row_sum, weighted = attend_pair(
            query[:, at], own_keys[:, at], own_values[:, at], None, lanes
        )
        weighted_out[:, at] = jnp.where(low, weighted[:COLS], weighted[COLS:])
        for half in range(2):
            head = 2 * pair + half
            at_rows = slice(half * COLS, (half + 1) * COLS)
            stats = jnp.where(lanes == head, row_max[at_rows], stats)
            stats = jnp.where(lanes == HEADS + head, row_sum[at_rows], stats)
    stats_out[...] = stats


def finish_kernel(partial, fresh, fresh_stats, wo, attended, convolved):
    total = jnp.zeros((COLS, CO), F32)
    for d in range(GROUP):
        total += partial[d, :, D : D + CO].astype(F32)
    convolved[...] = total.astype(BF16)
    stats = []
    for d in range(GROUP):
        packed = partial[d, :, D + 2 * LANES :].astype(F32)
        terms = sum(pltpu.roll(packed, LANES - at, 1) for at in STATS_AT)
        stats.append(jnp.where(lane_ids(COLS) < 2 * HEADS, terms, 0.0))
    stats.append(fresh_stats[...])
    top = stats[0]
    for s in stats[1:]:
        top = jnp.maximum(top, s)
    scale = [jnp.exp(s - top) for s in stats]
    sums = [pltpu.roll(s, LANES - HEADS, 1) for s in stats]
    parts = [scale[d] * sums[d] for d in range(GROUP)]
    whole = scale[GROUP] * sums[GROUP]
    for p in parts:
        whole = whole + p
    weights = [p / whole for p in parts] + [scale[GROUP] / whole]
    low = lane_ids(COLS) < HEAD_DIM
    mixed = []
    for pair in range(PAIRS):
        at = slice(pair * LANES, (pair + 1) * LANES)
        sum_pair = jnp.zeros((COLS, LANES), F32)
        for d in range(GROUP + 1):
            w = jnp.where(
                low, weights[d][:, 2 * pair : 2 * pair + 1], weights[d][:, 2 * pair + 1 : 2 * pair + 2]
            )
            sum_pair += w * (partial[d, :, at].astype(F32) if d < GROUP else fresh[:, at])
        mixed.append(sum_pair.astype(BF16))
    attended[...] = dot(jnp.concatenate(mixed, axis=1), wo[...]).astype(BF16)


ANY_SPEC = pl.BlockSpec(memory_space=pl.ANY)
VMEM_SPEC = pl.BlockSpec(memory_space=pltpu.VMEM)
HBM_SPEC = pl.BlockSpec(memory_space=pltpu.HBM)


def params():
    return pltpu.CompilerParams(vmem_limit_bytes=VMEM)


def cost(us):
    return pl.CostEstimate(flops=int(us * 1e9), bytes_accessed=0, transcendentals=0)


def shape(dims, dtype=BF16):
    return jax.ShapeDtypeStruct(dims, dtype)


def local(block_input, stale_input, query_weight, key_weight, value_weight, out_weight, conv_weight):
    block = block_input.reshape(COLS, D)
    stale = stale_input.reshape(COLS, D)
    with jax.named_scope("payload"):
        payload = pl.pallas_call(
            payload_kernel,
            out_shape=shape((COLS + 16, D)),
            in_specs=[HBM_SPEC] * 2,
            scratch_shapes=[
                pltpu.VMEM((COLS, D), BF16),
                pltpu.VMEM((9, OWN, CO), BF16),
                pltpu.VMEM((16, D), F32),
                pltpu.SemaphoreType.DMA((2,)),
            ],
            compiler_params=params(),
            cost_estimate=cost(PAYLOAD),
        )(stale, conv_weight)
    gathered = lax.all_gather(payload, "z", axis=0)
    with jax.named_scope("prepare"):
        send, query = pl.pallas_call(
            prepare_kernel,
            out_shape=(shape((GROUP, COLS, SEND)), shape((COLS, D))),
            compiler_params=params(),
            cost_estimate=cost(PREPARE),
        )(block, gathered, query_weight, jnp.asarray(slice_matrix()))
    sent = lax.all_to_all(send, ("yh", "x"), 0, 0, tiled=True)
    other = lax.ppermute(gathered[:, COLS:, :], "core", [(0, 1), (1, 0)])
    sides = []
    for name, weight in (("keys", key_weight), ("values", value_weight)):
        with jax.named_scope(name):
            sides.append(
                pl.pallas_call(
                    project_kernel,
                    out_shape=(shape((KEYS, D)), shape((COLS, D))),
                    in_specs=[VMEM_SPEC] * 3 + [ANY_SPEC],
                    compiler_params=params(),
                    cost_estimate=cost(PROJECT),
                )(gathered, block, weight, sides[0][0] if sides else send)
            )
    (keys, own_keys), (values, own_values) = sides
    with jax.named_scope("attend"):
        back = pl.pallas_call(
            attend_kernel,
            out_shape=shape((GROUP, COLS, BACK)),
            compiler_params=params(),
            cost_estimate=cost(ATTEND),
        )(sent, keys, values, gathered, other)
    partial = lax.all_to_all(back, ("yh", "x"), 0, 0, tiled=True)
    with jax.named_scope("fresh"):
        fresh, fresh_stats = pl.pallas_call(
            fresh_kernel,
            out_shape=(shape((COLS, D), F32), shape((COLS, LANES), F32)),
            in_specs=[VMEM_SPEC] * 3 + [ANY_SPEC],
            compiler_params=params(),
            cost_estimate=cost(FRESH),
        )(own_keys, own_values, query, back)
    with jax.named_scope("finish"):
        attended, convolved = pl.pallas_call(
            finish_kernel,
            out_shape=(shape((COLS, D)), shape((COLS, CO))),
            compiler_params=params(),
            cost_estimate=cost(FINISH),
        )(partial, fresh, fresh_stats, out_weight)
    return attended.reshape(1, COLS, D), convolved.reshape(1, COLS, CO)


def solution(mesh):
    axes = Mesh(mesh.devices.reshape(Z, 2, 4, 2, 2), ("z", "yh", "x", "yl", "core"))
    rows, batch = ("z", "yh", "x"), ("yl", "core")
    placed = P(rows, batch, None)
    return jax.shard_map(
        local,
        mesh=axes,
        in_specs=(placed, placed, P(), P(), P(), P(), P(None, rows, None)),
        out_specs=(placed, placed),
        check_vma=False,
    )
```

```python
import jax
import jax.numpy as jnp
import ml_dtypes
import numpy as np
from jax import lax
from jax.experimental import pallas as pl
from jax.experimental.pallas import tpu as pltpu
from jax.sharding import Mesh, PartitionSpec as P

HEADS = 10
HEAD_DIM = 64
D = 640
CO = 320
COLS = 32
Z = 16
GROUP = 8
OWN = 5
LANES = 128
PAIRS = HEADS // 2
QUERIES = GROUP * COLS
KEYS = Z * COLS
SEND = D + 3 * LANES
BACK = D + 3 * LANES
VMEM = 24 * 1024 * 1024
PAYLOAD, PREPARE, PROJECT, ATTEND, FRESH, FINISH = 1, 2, 1, 3, 0.2, 2
STATS_AT = (64, 84, 104)
F32 = jnp.float32
BF16 = jnp.bfloat16


def slice_matrix():
    out = np.zeros((D, GROUP * LANES), np.float32)
    for j in range(GROUP):
        for z in range(Z):
            for c in range(OWN):
                out[(z * GROUP + j) * OWN + c, LANES * j + 8 * z + c] = 1.0
    return out.astype(ml_dtypes.bfloat16)


def tap_matrix():
    row = lax.broadcasted_iota(jnp.int32, (3 * LANES, 2 * LANES), 0)
    col = lax.broadcasted_iota(jnp.int32, (3 * LANES, 2 * LANES), 1)
    z, c = (row % LANES) // 8, row % 8
    target = 16 * z + OWN * (row // LANES) + c
    return jnp.where((c < OWN) & (col == target), 1.0, 0.0).astype(BF16)


def layer_norm(values_in):
    mean = jnp.mean(values_in, axis=-1, keepdims=True)
    centered = values_in - mean
    variance = jnp.mean(centered * centered, axis=-1, keepdims=True)
    return (centered * lax.rsqrt(variance + 1e-05)).astype(BF16)


def silu(values_in):
    return (values_in * jax.nn.sigmoid(values_in)).astype(BF16)


def dot(a, b):
    return jnp.dot(a, b, preferred_element_type=F32)


def dot_t(a, b):
    return lax.dot_general(a, b, (((1,), (1,)), ((), ())), preferred_element_type=F32)


def lane_ids(rows):
    return lax.broadcasted_iota(jnp.int32, (rows, LANES), 1)


def place():
    return lax.axis_index("z"), lax.axis_index("yh") * 4 + lax.axis_index("x")


def payload_kernel(stale_hbm, taps_hbm, gather, stale, taps, rows, sems):
    copies = [
        pltpu.make_async_copy(taps_hbm, taps, sems.at[0]),
        pltpu.make_async_copy(stale_hbm, stale, sems.at[1]),
    ]
    for copy in copies:
        copy.start()
    core = lax.axis_index("core")
    rows[...] = jnp.zeros_like(rows)
    copies[0].wait()
    for dx in range(3):
        first = jnp.where(core == 0, taps[dx].astype(F32), taps[6 + dx].astype(F32))
        second = jnp.where(core == 0, taps[3 + dx].astype(F32), 0.0)
        rows[OWN * dx : OWN * (dx + 1), :] = jnp.concatenate([first, second], axis=1)
    gather[COLS:, :] = rows[...].astype(BF16)
    copies[1].wait()
    gather[:COLS, :] = stale[...]


def prepare_kernel(block, gathered, wq, slices, send, query_out):
    z, j = place()
    beside = jnp.where(j == 0, jnp.minimum(z + 1, Z - 1), jnp.maximum(z - 1, 0))
    stale = gathered[z, :COLS, :]
    query = dot(layer_norm(block[...].astype(F32)), wq[...]).astype(BF16)
    query = query * jnp.array(HEAD_DIM**-0.5, BF16)
    query_out[...] = query
    outside = ((j == 0) & (z == Z - 1)) | ((j != 0) & (z == 0))
    halo = gathered[beside, :COLS, :].astype(F32) * jnp.where(outside, 0.0, 1.0)
    three = jnp.concatenate(
        [silu(block[...].astype(F32)), silu(stale.astype(F32)), silu(halo)], axis=0
    )
    cut = dot(three, slices[...]).astype(BF16)
    for j in range(GROUP):
        send[j, :, :D] = query
        for part in range(3):
            send[j, :, D + part * LANES : D + (part + 1) * LANES] = cut[
                part * COLS : (part + 1) * COLS, j * LANES : (j + 1) * LANES
            ]


def project_kernel(gathered, block, weight, after, out, own):
    del after
    normed = layer_norm(gathered[:, :COLS, :].reshape(KEYS, D).astype(F32))
    fresh = layer_norm(block[...].astype(F32))
    out[...] = dot(normed, weight[...]).astype(BF16)
    own[...] = dot(fresh, weight[...]).astype(BF16)


def attend_pair(query, keys, values, masked, lanes):
    low = lanes < HEAD_DIM
    zero = jnp.zeros_like(query)
    two = jnp.concatenate([jnp.where(low, query, zero), jnp.where(low, zero, query)], axis=0)
    if masked is not None:
        two = jnp.concatenate([two, masked[0]], axis=1)
        keys = jnp.concatenate([keys, masked[1]], axis=1)
    scores = dot_t(two, keys)
    row_max = jnp.max(scores, axis=-1, keepdims=True)
    exp_scores = jnp.exp(scores - row_max)
    row_sum = jnp.sum(exp_scores, axis=-1, keepdims=True)
    weighted = dot(exp_scores.astype(BF16), values)
    return row_max, row_sum, weighted


def convolve(sent, gathered, other):
    spread = tap_matrix()
    mine = gathered[:, COLS:, :].reshape(Z * 16, D)
    theirs = other[...].reshape(Z * 16, D)
    zero_core = lax.axis_index("core") == 0
    lower_half = jnp.where(zero_core, mine, theirs)
    upper_half = jnp.where(zero_core, theirs, mine)
    weights = (lower_half[:, :CO], lower_half[:, CO:], upper_half[:, :CO])
    active = sent[:, :, D : D + LANES]
    stale = sent[:, :, D + LANES : D + 2 * LANES]
    upper = jnp.concatenate([sent[7:8, :, D + 2 * LANES :], stale[:7]], axis=0)
    lower = jnp.concatenate([stale[1:], sent[0:1, :, D + 2 * LANES :]], axis=0)
    column = lax.broadcasted_iota(jnp.int32, (QUERIES, LANES), 0) % COLS
    total = jnp.zeros((QUERIES, CO), F32)
    for dy, source in enumerate((upper, active, lower)):
        rows = source.reshape(QUERIES, LANES).astype(F32)
        left = jnp.where(column == 0, 0.0, pltpu.roll(rows, 1, 0))
        right = jnp.where(column == COLS - 1, 0.0, pltpu.roll(rows, QUERIES - 1, 0))
        three = jnp.concatenate([left.astype(BF16), rows.astype(BF16), right.astype(BF16)], axis=1)
        total += dot(dot(three, spread).astype(BF16), weights[dy])
    return total


def attend_kernel(sent, all_keys, all_values, gathered, other, after, back):
    del after
    z, j = place()
    rows = lax.broadcasted_iota(jnp.int32, (2 * QUERIES, LANES), 0)
    here = lax.broadcasted_iota(jnp.int32, (2 * QUERIES, LANES), 1) == 0
    own_query = jnp.where(here & (((rows // COLS) % GROUP) == j), -1e30, 0.0).astype(BF16)
    own_key = jnp.where(here & ((rows // COLS) == z), 1.0, 0.0).astype(BF16)
    masked = (own_query, own_key)
    lanes = lane_ids(QUERIES)
    low = lanes < HEAD_DIM
    stats = jnp.zeros((QUERIES, LANES), F32)
    for pair in range(PAIRS):
        at = slice(pair * LANES, (pair + 1) * LANES)
        query = sent[:, :, at].reshape(QUERIES, LANES)
        keys, values = all_keys[:, at], all_values[:, at]
        row_max, row_sum, weighted = attend_pair(query, keys, values, masked, lanes)
        weighted = weighted / row_sum
        mixed = jnp.where(low, weighted[:QUERIES], weighted[QUERIES:])
        back[:, :, at] = mixed.astype(BF16).reshape(GROUP, COLS, LANES)
        for half in range(2):
            head = 2 * pair + half
            at_rows = slice(half * QUERIES, (half + 1) * QUERIES)
            stats = jnp.where(lanes == head, row_max[at_rows], stats)
            stats = jnp.where(lanes == HEADS + head, row_sum[at_rows], stats)
    high = stats.astype(BF16).astype(F32)
    rest = stats - high
    middle = rest.astype(BF16).astype(F32)
    last = rest - middle
    packed = sum(pltpu.roll(term, at, 1) for term, at in zip((high, middle, last), STATS_AT))
    total = convolve(sent, gathered, other)
    back[:, :, D : D + 2 * LANES] = (
        total[:, : 2 * LANES].astype(BF16).reshape(GROUP, COLS, 2 * LANES)
    )
    tail = jnp.concatenate([total[:, 2 * LANES :], packed[:, CO - 2 * LANES :]], axis=1)
    back[:, :, D + 2 * LANES :] = tail.astype(BF16).reshape(GROUP, COLS, LANES)


def fresh_kernel(own_keys, own_values, query, weighted_out, stats_out):
    lanes = lane_ids(COLS)
    low = lanes < HEAD_DIM
    stats = jnp.zeros((COLS, LANES), F32)
    for pair in range(PAIRS):
        at = slice(pair * LANES, (pair + 1) * LANES)
        row_max, row_sum, weighted = attend_pair(
            query[:, at], own_keys[:, at], own_values[:, at], None, lanes
        )
        weighted_out[:, at] = jnp.where(low, weighted[:COLS], weighted[COLS:])
        for half in range(2):
            head = 2 * pair + half
            at_rows = slice(half * COLS, (half + 1) * COLS)
            stats = jnp.where(lanes == head, row_max[at_rows], stats)
            stats = jnp.where(lanes == HEADS + head, row_sum[at_rows], stats)
    stats_out[...] = stats


def finish_kernel(partial, fresh, fresh_stats, wo, attended, convolved):
    total = jnp.zeros((COLS, CO), F32)
    for d in range(GROUP):
        total += partial[d, :, D : D + CO].astype(F32)
    convolved[...] = total.astype(BF16)
    stats = []
    for d in range(GROUP):
        packed = partial[d, :, D + 2 * LANES :].astype(F32)
        terms = sum(pltpu.roll(packed, LANES - at, 1) for at in STATS_AT)
        stats.append(jnp.where(lane_ids(COLS) < 2 * HEADS, terms, 0.0))
    stats.append(fresh_stats[...])
    top = stats[0]
    for s in stats[1:]:
        top = jnp.maximum(top, s)
    scale = [jnp.exp(s - top) for s in stats]
    sums = [pltpu.roll(s, LANES - HEADS, 1) for s in stats]
    parts = [scale[d] * sums[d] for d in range(GROUP)]
    whole = scale[GROUP] * sums[GROUP]
    for p in parts:
        whole = whole + p
    weights = [p / whole for p in parts] + [scale[GROUP] / whole]
    low = lane_ids(COLS) < HEAD_DIM
    mixed = []
    for pair in range(PAIRS):
        at = slice(pair * LANES, (pair + 1) * LANES)
        sum_pair = jnp.zeros((COLS, LANES), F32)
        for d in range(GROUP + 1):
            w = jnp.where(
                low, weights[d][:, 2 * pair : 2 * pair + 1], weights[d][:, 2 * pair + 1 : 2 * pair + 2]
            )
            sum_pair += w * (partial[d, :, at].astype(F32) if d < GROUP else fresh[:, at])
        mixed.append(sum_pair.astype(BF16))
    attended[...] = dot(jnp.concatenate(mixed, axis=1), wo[...]).astype(BF16)


ANY_SPEC = pl.BlockSpec(memory_space=pl.ANY)
VMEM_SPEC = pl.BlockSpec(memory_space=pltpu.VMEM)
HBM_SPEC = pl.BlockSpec(memory_space=pltpu.HBM)


def params():
    return pltpu.CompilerParams(vmem_limit_bytes=VMEM)


def cost(us):
    return pl.CostEstimate(flops=int(us * 1e9), bytes_accessed=0, transcendentals=0)


def shape(dims, dtype=BF16):
    return jax.ShapeDtypeStruct(dims, dtype)


def local(block_input, stale_input, query_weight, key_weight, value_weight, out_weight, conv_weight):
    block = block_input.reshape(COLS, D)
    stale = stale_input.reshape(COLS, D)
    with jax.named_scope("payload"):
        payload = pl.pallas_call(
            payload_kernel,
            out_shape=shape((COLS + 16, D)),
            in_specs=[HBM_SPEC] * 2,
            scratch_shapes=[
                pltpu.VMEM((COLS, D), BF16),
                pltpu.VMEM((9, OWN, CO), BF16),
                pltpu.VMEM((16, D), F32),
                pltpu.SemaphoreType.DMA((2,)),
            ],
            compiler_params=params(),
            cost_estimate=cost(PAYLOAD),
        )(stale, conv_weight)
    gathered = lax.all_gather(payload, "z", axis=0)
    with jax.named_scope("prepare"):
        send, query = pl.pallas_call(
            prepare_kernel,
            out_shape=(shape((GROUP, COLS, SEND)), shape((COLS, D))),
            compiler_params=params(),
            cost_estimate=cost(PREPARE),
        )(block, gathered, query_weight, jnp.asarray(slice_matrix()))
    sent = lax.all_to_all(send, ("yh", "x"), 0, 0, tiled=True)
    other = lax.ppermute(gathered[:, COLS:, :], "core", [(0, 1), (1, 0)])
    sides = []
    for name, weight in (("keys", key_weight), ("values", value_weight)):
        with jax.named_scope(name):
            sides.append(
                pl.pallas_call(
                    project_kernel,
                    out_shape=(shape((KEYS, D)), shape((COLS, D))),
                    in_specs=[VMEM_SPEC] * 3 + [ANY_SPEC],
                    compiler_params=params(),
                    cost_estimate=cost(PROJECT),
                )(gathered, block, weight, sides[0][0] if sides else send)
            )
    (keys, own_keys), (values, own_values) = sides
    with jax.named_scope("fresh"):
        fresh, fresh_stats = pl.pallas_call(
            fresh_kernel,
            out_shape=(shape((COLS, D), F32), shape((COLS, LANES), F32)),
            compiler_params=params(),
            cost_estimate=cost(FRESH),
        )(own_keys, own_values, query)
    with jax.named_scope("attend"):
        back = pl.pallas_call(
            attend_kernel,
            out_shape=shape((GROUP, COLS, BACK)),
            in_specs=[VMEM_SPEC] * 5 + [ANY_SPEC],
            compiler_params=params(),
            cost_estimate=cost(ATTEND),
        )(sent, keys, values, gathered, other, fresh_stats)
    partial = lax.all_to_all(back, ("yh", "x"), 0, 0, tiled=True)
    with jax.named_scope("finish"):
        attended, convolved = pl.pallas_call(
            finish_kernel,
            out_shape=(shape((COLS, D)), shape((COLS, CO))),
            compiler_params=params(),
            cost_estimate=cost(FINISH),
        )(partial, fresh, fresh_stats, out_weight)
    return attended.reshape(1, COLS, D), convolved.reshape(1, COLS, CO)


def solution(mesh):
    axes = Mesh(mesh.devices.reshape(Z, 2, 4, 2, 2), ("z", "yh", "x", "yl", "core"))
    rows, batch = ("z", "yh", "x"), ("yl", "core")
    placed = P(rows, batch, None)
    return jax.shard_map(
        local,
        mesh=axes,
        in_specs=(placed, placed, P(), P(), P(), P(), P(None, rows, None)),
        out_specs=(placed, placed),
        check_vma=False,
    )
```

```python
import jax
import jax.numpy as jnp
import ml_dtypes
import numpy as np
from jax import lax
from jax.experimental import pallas as pl
from jax.experimental.pallas import tpu as pltpu
from jax.sharding import Mesh, PartitionSpec as P

HEADS = 10
HEAD_DIM = 64
D = 640
CO = 320
COLS = 32
Z = 16
GROUP = 8
OWN = 5
LANES = 128
PAIRS = HEADS // 2
QUERIES = GROUP * COLS
KEYS = Z * COLS
SEND = D + 3 * LANES
BACK = D + 3 * LANES
VMEM = 24 * 1024 * 1024
PAYLOAD, PREPARE, PROJECT, ATTEND, FRESH, FINISH = 1, 2, 1, 3, 0.2, 2
AHEAD = 3
STATS_AT = (64, 84, 104)
F32 = jnp.float32
BF16 = jnp.bfloat16


def slice_matrix():
    out = np.zeros((D, GROUP * LANES), np.float32)
    for j in range(GROUP):
        for z in range(Z):
            for c in range(OWN):
                out[(z * GROUP + j) * OWN + c, LANES * j + 8 * z + c] = 1.0
    return out.astype(ml_dtypes.bfloat16)


def tap_matrix():
    row = lax.broadcasted_iota(jnp.int32, (3 * LANES, 2 * LANES), 0)
    col = lax.broadcasted_iota(jnp.int32, (3 * LANES, 2 * LANES), 1)
    z, c = (row % LANES) // 8, row % 8
    target = 16 * z + OWN * (row // LANES) + c
    return jnp.where((c < OWN) & (col == target), 1.0, 0.0).astype(BF16)


def layer_norm(values_in):
    mean = jnp.mean(values_in, axis=-1, keepdims=True)
    centered = values_in - mean
    variance = jnp.mean(centered * centered, axis=-1, keepdims=True)
    return (centered * lax.rsqrt(variance + 1e-05)).astype(BF16)


def silu(values_in):
    return (values_in * jax.nn.sigmoid(values_in)).astype(BF16)


def dot(a, b):
    return jnp.dot(a, b, preferred_element_type=F32)


def dot_t(a, b):
    return lax.dot_general(a, b, (((1,), (1,)), ((), ())), preferred_element_type=F32)


def lane_ids(rows):
    return lax.broadcasted_iota(jnp.int32, (rows, LANES), 1)


def place():
    return lax.axis_index("z"), lax.axis_index("yh") * 4 + lax.axis_index("x")


def ahead_kernel(out):
    out[...] = jnp.zeros_like(out)


def payload_kernel(stale_hbm, taps_hbm, after, gather, stale, taps, rows, sems):
    del after
    copies = [
        pltpu.make_async_copy(taps_hbm, taps, sems.at[0]),
        pltpu.make_async_copy(stale_hbm, stale, sems.at[1]),
    ]
    for copy in copies:
        copy.start()
    core = lax.axis_index("core")
    rows[...] = jnp.zeros_like(rows)
    copies[0].wait()
    for dx in range(3):
        first = jnp.where(core == 0, taps[dx].astype(F32), taps[6 + dx].astype(F32))
        second = jnp.where(core == 0, taps[3 + dx].astype(F32), 0.0)
        rows[OWN * dx : OWN * (dx + 1), :] = jnp.concatenate([first, second], axis=1)
    gather[COLS:, :] = rows[...].astype(BF16)
    copies[1].wait()
    gather[:COLS, :] = stale[...]


def prepare_kernel(block, gathered, wq, slices, send, query_out):
    z, j = place()
    beside = jnp.where(j == 0, jnp.minimum(z + 1, Z - 1), jnp.maximum(z - 1, 0))
    stale = gathered[z, :COLS, :]
    query = dot(layer_norm(block[...].astype(F32)), wq[...]).astype(BF16)
    query = query * jnp.array(HEAD_DIM**-0.5, BF16)
    query_out[...] = query
    outside = ((j == 0) & (z == Z - 1)) | ((j != 0) & (z == 0))
    halo = gathered[beside, :COLS, :].astype(F32) * jnp.where(outside, 0.0, 1.0)
    three = jnp.concatenate(
        [silu(block[...].astype(F32)), silu(stale.astype(F32)), silu(halo)], axis=0
    )
    cut = dot(three, slices[...]).astype(BF16)
    for j in range(GROUP):
        send[j, :, :D] = query
        for part in range(3):
            send[j, :, D + part * LANES : D + (part + 1) * LANES] = cut[
                part * COLS : (part + 1) * COLS, j * LANES : (j + 1) * LANES
            ]


def project_kernel(gathered, block, weight, after, out, own):
    del after
    normed = layer_norm(gathered[:, :COLS, :].reshape(KEYS, D).astype(F32))
    fresh = layer_norm(block[...].astype(F32))
    out[...] = dot(normed, weight[...]).astype(BF16)
    own[...] = dot(fresh, weight[...]).astype(BF16)


def attend_pair(query, keys, values, masked, lanes):
    low = lanes < HEAD_DIM
    zero = jnp.zeros_like(query)
    two = jnp.concatenate([jnp.where(low, query, zero), jnp.where(low, zero, query)], axis=0)
    if masked is not None:
        two = jnp.concatenate([two, masked[0]], axis=1)
        keys = jnp.concatenate([keys, masked[1]], axis=1)
    scores = dot_t(two, keys)
    row_max = jnp.max(scores, axis=-1, keepdims=True)
    exp_scores = jnp.exp(scores - row_max)
    row_sum = jnp.sum(exp_scores, axis=-1, keepdims=True)
    weighted = dot(exp_scores.astype(BF16), values)
    return row_max, row_sum, weighted


def convolve(sent, gathered, other):
    spread = tap_matrix()
    mine = gathered[:, COLS:, :].reshape(Z * 16, D)
    theirs = other[...].reshape(Z * 16, D)
    zero_core = lax.axis_index("core") == 0
    lower_half = jnp.where(zero_core, mine, theirs)
    upper_half = jnp.where(zero_core, theirs, mine)
    weights = (lower_half[:, :CO], lower_half[:, CO:], upper_half[:, :CO])
    active = sent[:, :, D : D + LANES]
    stale = sent[:, :, D + LANES : D + 2 * LANES]
    upper = jnp.concatenate([sent[7:8, :, D + 2 * LANES :], stale[:7]], axis=0)
    lower = jnp.concatenate([stale[1:], sent[0:1, :, D + 2 * LANES :]], axis=0)
    column = lax.broadcasted_iota(jnp.int32, (QUERIES, LANES), 0) % COLS
    total = jnp.zeros((QUERIES, CO), F32)
    for dy, source in enumerate((upper, active, lower)):
        rows = source.reshape(QUERIES, LANES).astype(F32)
        left = jnp.where(column == 0, 0.0, pltpu.roll(rows, 1, 0))
        right = jnp.where(column == COLS - 1, 0.0, pltpu.roll(rows, QUERIES - 1, 0))
        three = jnp.concatenate([left.astype(BF16), rows.astype(BF16), right.astype(BF16)], axis=1)
        total += dot(dot(three, spread).astype(BF16), weights[dy])
    return total


def attend_kernel(sent, all_keys, all_values, gathered, other, after, back):
    del after
    z, j = place()
    rows = lax.broadcasted_iota(jnp.int32, (2 * QUERIES, LANES), 0)
    here = lax.broadcasted_iota(jnp.int32, (2 * QUERIES, LANES), 1) == 0
    own_query = jnp.where(here & (((rows // COLS) % GROUP) == j), -1e30, 0.0).astype(BF16)
    own_key = jnp.where(here & ((rows // COLS) == z), 1.0, 0.0).astype(BF16)
    masked = (own_query, own_key)
    lanes = lane_ids(QUERIES)
    low = lanes < HEAD_DIM
    stats = jnp.zeros((QUERIES, LANES), F32)
    for pair in range(PAIRS):
        at = slice(pair * LANES, (pair + 1) * LANES)
        query = sent[:, :, at].reshape(QUERIES, LANES)
        keys, values = all_keys[:, at], all_values[:, at]
        row_max, row_sum, weighted = attend_pair(query, keys, values, masked, lanes)
        weighted = weighted / row_sum
        mixed = jnp.where(low, weighted[:QUERIES], weighted[QUERIES:])
        back[:, :, at] = mixed.astype(BF16).reshape(GROUP, COLS, LANES)
        for half in range(2):
            head = 2 * pair + half
            at_rows = slice(half * QUERIES, (half + 1) * QUERIES)
            stats = jnp.where(lanes == head, row_max[at_rows], stats)
            stats = jnp.where(lanes == HEADS + head, row_sum[at_rows], stats)
    high = stats.astype(BF16).astype(F32)
    rest = stats - high
    middle = rest.astype(BF16).astype(F32)
    last = rest - middle
    packed = sum(pltpu.roll(term, at, 1) for term, at in zip((high, middle, last), STATS_AT))
    total = convolve(sent, gathered, other)
    back[:, :, D : D + 2 * LANES] = (
        total[:, : 2 * LANES].astype(BF16).reshape(GROUP, COLS, 2 * LANES)
    )
    tail = jnp.concatenate([total[:, 2 * LANES :], packed[:, CO - 2 * LANES :]], axis=1)
    back[:, :, D + 2 * LANES :] = tail.astype(BF16).reshape(GROUP, COLS, LANES)


def fresh_kernel(own_keys, own_values, query, weighted_out, stats_out):
    lanes = lane_ids(COLS)
    low = lanes < HEAD_DIM
    stats = jnp.zeros((COLS, LANES), F32)
    for pair in range(PAIRS):
        at = slice(pair * LANES, (pair + 1) * LANES)
        row_max, row_sum, weighted = attend_pair(
            query[:, at], own_keys[:, at], own_values[:, at], None, lanes
        )
        weighted_out[:, at] = jnp.where(low, weighted[:COLS], weighted[COLS:])
        for half in range(2):
            head = 2 * pair + half
            at_rows = slice(half * COLS, (half + 1) * COLS)
            stats = jnp.where(lanes == head, row_max[at_rows], stats)
            stats = jnp.where(lanes == HEADS + head, row_sum[at_rows], stats)
    stats_out[...] = stats


def finish_kernel(partial, fresh, fresh_stats, wo, attended, convolved):
    total = jnp.zeros((COLS, CO), F32)
    for d in range(GROUP):
        total += partial[d, :, D : D + CO].astype(F32)
    convolved[...] = total.astype(BF16)
    stats = []
    for d in range(GROUP):
        packed = partial[d, :, D + 2 * LANES :].astype(F32)
        terms = sum(pltpu.roll(packed, LANES - at, 1) for at in STATS_AT)
        stats.append(jnp.where(lane_ids(COLS) < 2 * HEADS, terms, 0.0))
    stats.append(fresh_stats[...])
    top = stats[0]
    for s in stats[1:]:
        top = jnp.maximum(top, s)
    scale = [jnp.exp(s - top) for s in stats]
    sums = [pltpu.roll(s, LANES - HEADS, 1) for s in stats]
    parts = [scale[d] * sums[d] for d in range(GROUP)]
    whole = scale[GROUP] * sums[GROUP]
    for p in parts:
        whole = whole + p
    weights = [p / whole for p in parts] + [scale[GROUP] / whole]
    low = lane_ids(COLS) < HEAD_DIM
    mixed = []
    for pair in range(PAIRS):
        at = slice(pair * LANES, (pair + 1) * LANES)
        sum_pair = jnp.zeros((COLS, LANES), F32)
        for d in range(GROUP + 1):
            w = jnp.where(
                low, weights[d][:, 2 * pair : 2 * pair + 1], weights[d][:, 2 * pair + 1 : 2 * pair + 2]
            )
            sum_pair += w * (partial[d, :, at].astype(F32) if d < GROUP else fresh[:, at])
        mixed.append(sum_pair.astype(BF16))
    attended[...] = dot(jnp.concatenate(mixed, axis=1), wo[...]).astype(BF16)


ANY_SPEC = pl.BlockSpec(memory_space=pl.ANY)
VMEM_SPEC = pl.BlockSpec(memory_space=pltpu.VMEM)
HBM_SPEC = pl.BlockSpec(memory_space=pltpu.HBM)


def params():
    return pltpu.CompilerParams(vmem_limit_bytes=VMEM)


def cost(us):
    return pl.CostEstimate(flops=int(us * 1e9), bytes_accessed=0, transcendentals=0)


def shape(dims, dtype=BF16):
    return jax.ShapeDtypeStruct(dims, dtype)


def local(block_input, stale_input, query_weight, key_weight, value_weight, out_weight, conv_weight):
    block = block_input.reshape(COLS, D)
    stale = stale_input.reshape(COLS, D)
    with jax.named_scope("ahead"):
        ahead = pl.pallas_call(
            ahead_kernel,
            out_shape=shape((8, LANES), F32),
            compiler_params=params(),
            cost_estimate=cost(AHEAD),
        )()
    with jax.named_scope("payload"):
        payload = pl.pallas_call(
            payload_kernel,
            out_shape=shape((COLS + 16, D)),
            in_specs=[HBM_SPEC] * 2 + [ANY_SPEC],
            scratch_shapes=[
                pltpu.VMEM((COLS, D), BF16),
                pltpu.VMEM((9, OWN, CO), BF16),
                pltpu.VMEM((16, D), F32),
                pltpu.SemaphoreType.DMA((2,)),
            ],
            compiler_params=params(),
            cost_estimate=cost(PAYLOAD),
        )(stale, conv_weight, ahead)
    gathered = lax.all_gather(payload, "z", axis=0)
    with jax.named_scope("prepare"):
        send, query = pl.pallas_call(
            prepare_kernel,
            out_shape=(shape((GROUP, COLS, SEND)), shape((COLS, D))),
            compiler_params=params(),
            cost_estimate=cost(PREPARE),
        )(block, gathered, query_weight, jnp.asarray(slice_matrix()))
    sent = lax.all_to_all(send, ("yh", "x"), 0, 0, tiled=True)
    other = lax.ppermute(gathered[:, COLS:, :], "core", [(0, 1), (1, 0)])
    sides = []
    for name, weight in (("keys", key_weight), ("values", value_weight)):
        with jax.named_scope(name):
            sides.append(
                pl.pallas_call(
                    project_kernel,
                    out_shape=(shape((KEYS, D)), shape((COLS, D))),
                    in_specs=[VMEM_SPEC] * 3 + [ANY_SPEC],
                    compiler_params=params(),
                    cost_estimate=cost(PROJECT),
                )(gathered, block, weight, sides[0][0] if sides else send)
            )
    (keys, own_keys), (values, own_values) = sides
    with jax.named_scope("fresh"):
        fresh, fresh_stats = pl.pallas_call(
            fresh_kernel,
            out_shape=(shape((COLS, D), F32), shape((COLS, LANES), F32)),
            compiler_params=params(),
            cost_estimate=cost(FRESH),
        )(own_keys, own_values, query)
    with jax.named_scope("attend"):
        back = pl.pallas_call(
            attend_kernel,
            out_shape=shape((GROUP, COLS, BACK)),
            in_specs=[VMEM_SPEC] * 5 + [ANY_SPEC],
            compiler_params=params(),
            cost_estimate=cost(ATTEND),
        )(sent, keys, values, gathered, other, fresh_stats)
    partial = lax.all_to_all(back, ("yh", "x"), 0, 0, tiled=True)
    with jax.named_scope("finish"):
        attended, convolved = pl.pallas_call(
            finish_kernel,
            out_shape=(shape((COLS, D)), shape((COLS, CO))),
            compiler_params=params(),
            cost_estimate=cost(FINISH),
        )(partial, fresh, fresh_stats, out_weight)
    return attended.reshape(1, COLS, D), convolved.reshape(1, COLS, CO)


def solution(mesh):
    axes = Mesh(mesh.devices.reshape(Z, 2, 4, 2, 2), ("z", "yh", "x", "yl", "core"))
    rows, batch = ("z", "yh", "x"), ("yl", "core")
    placed = P(rows, batch, None)
    return jax.shard_map(
        local,
        mesh=axes,
        in_specs=(placed, placed, P(), P(), P(), P(), P(None, rows, None)),
        out_specs=(placed, placed),
        check_vma=False,
    )
```

```python
import jax
import jax.numpy as jnp
import ml_dtypes
import numpy as np
from jax import lax
from jax.experimental import pallas as pl
from jax.experimental.pallas import tpu as pltpu
from jax.sharding import Mesh, PartitionSpec as P

HEADS = 10
HEAD_DIM = 64
D = 640
CO = 320
COLS = 32
Z = 16
GROUP = 8
OWN = 5
LANES = 128
PAIRS = HEADS // 2
QUERIES = GROUP * COLS
KEYS = Z * COLS
SEND = D + 3 * LANES
BACK = D + 3 * LANES
VMEM = 24 * 1024 * 1024
PAYLOAD, PREPARE, PROJECT, ATTEND, FRESH, FINISH = 1, 2, 1, 3, 0.2, 2
AHEAD = 3
STATS_AT = (64, 84, 104)
F32 = jnp.float32
BF16 = jnp.bfloat16


def slice_matrix():
    out = np.zeros((D, GROUP * LANES), np.float32)
    for j in range(GROUP):
        for z in range(Z):
            for c in range(OWN):
                out[(z * GROUP + j) * OWN + c, LANES * j + 8 * z + c] = 1.0
    return out.astype(ml_dtypes.bfloat16)


def tap_matrix():
    row = lax.broadcasted_iota(jnp.int32, (3 * LANES, 2 * LANES), 0)
    col = lax.broadcasted_iota(jnp.int32, (3 * LANES, 2 * LANES), 1)
    z, c = (row % LANES) // 8, row % 8
    target = 16 * z + OWN * (row // LANES) + c
    return jnp.where((c < OWN) & (col == target), 1.0, 0.0).astype(BF16)


def layer_norm(values_in):
    mean = jnp.mean(values_in, axis=-1, keepdims=True)
    centered = values_in - mean
    variance = jnp.mean(centered * centered, axis=-1, keepdims=True)
    return (centered * lax.rsqrt(variance + 1e-05)).astype(BF16)


def silu(values_in):
    return (values_in * jax.nn.sigmoid(values_in)).astype(BF16)


def dot(a, b):
    return jnp.dot(a, b, preferred_element_type=F32)


def dot_t(a, b):
    return lax.dot_general(a, b, (((1,), (1,)), ((), ())), preferred_element_type=F32)


def lane_ids(rows):
    return lax.broadcasted_iota(jnp.int32, (rows, LANES), 1)


def place():
    return lax.axis_index("z"), lax.axis_index("yh") * 4 + lax.axis_index("x")


def ahead_kernel(out):
    out[...] = jnp.zeros_like(out)


def payload_kernel(stale_hbm, taps_hbm, after, gather, stale, taps, rows, sems):
    del after
    copies = [
        pltpu.make_async_copy(taps_hbm, taps, sems.at[0]),
        pltpu.make_async_copy(stale_hbm, stale, sems.at[1]),
    ]
    for copy in copies:
        copy.start()
    core = lax.axis_index("core")
    rows[...] = jnp.zeros_like(rows)
    copies[0].wait()
    for dx in range(3):
        first = jnp.where(core == 0, taps[dx].astype(F32), taps[6 + dx].astype(F32))
        second = jnp.where(core == 0, taps[3 + dx].astype(F32), 0.0)
        rows[OWN * dx : OWN * (dx + 1), :] = jnp.concatenate([first, second], axis=1)
    gather[COLS:, :] = rows[...].astype(BF16)
    copies[1].wait()
    gather[:COLS, :] = stale[...]


def prepare_kernel(block, gathered, wq, slices, send, query_out):
    z, j = place()
    beside = jnp.where(j == 0, jnp.minimum(z + 1, Z - 1), jnp.maximum(z - 1, 0))
    stale = gathered[z, :COLS, :]
    query = dot(layer_norm(block[...].astype(F32)), wq[...]).astype(BF16)
    query = query * jnp.array(HEAD_DIM**-0.5, BF16)
    query_out[...] = query
    outside = ((j == 0) & (z == Z - 1)) | ((j != 0) & (z == 0))
    halo = gathered[beside, :COLS, :].astype(F32) * jnp.where(outside, 0.0, 1.0)
    three = jnp.concatenate(
        [silu(block[...].astype(F32)), silu(stale.astype(F32)), silu(halo)], axis=0
    )
    cut = dot(three, slices[...]).astype(BF16)
    for j in range(GROUP):
        send[j, :, :D] = query
        for part in range(3):
            send[j, :, D + part * LANES : D + (part + 1) * LANES] = cut[
                part * COLS : (part + 1) * COLS, j * LANES : (j + 1) * LANES
            ]


def project_kernel(gathered, block, weight, after, out, own):
    del after
    normed = layer_norm(gathered[:, :COLS, :].reshape(KEYS, D).astype(F32))
    fresh = layer_norm(block[...].astype(F32))
    out[...] = dot(normed, weight[...]).astype(BF16)
    own[...] = dot(fresh, weight[...]).astype(BF16)


def attend_pair(query, keys, values, masked, lanes):
    low = lanes < HEAD_DIM
    zero = jnp.zeros_like(query)
    two = jnp.concatenate([jnp.where(low, query, zero), jnp.where(low, zero, query)], axis=0)
    if masked is not None:
        two = jnp.concatenate([two, masked[0]], axis=1)
        keys = jnp.concatenate([keys, masked[1]], axis=1)
    scores = dot_t(two, keys)
    row_max = jnp.max(scores, axis=-1, keepdims=True)
    exp_scores = jnp.exp(scores - row_max)
    row_sum = jnp.sum(exp_scores, axis=-1, keepdims=True)
    weighted = dot(exp_scores.astype(BF16), values)
    return row_max, row_sum, weighted


def convolve(sent, gathered, other):
    spread = tap_matrix()
    mine = gathered[:, COLS:, :].reshape(Z * 16, D)
    theirs = other[...].reshape(Z * 16, D)
    zero_core = lax.axis_index("core") == 0
    lower_half = jnp.where(zero_core, mine, theirs)
    upper_half = jnp.where(zero_core, theirs, mine)
    weights = (lower_half[:, :CO], lower_half[:, CO:], upper_half[:, :CO])
    active = sent[:, :, D : D + LANES]
    stale = sent[:, :, D + LANES : D + 2 * LANES]
    upper = jnp.concatenate([sent[7:8, :, D + 2 * LANES :], stale[:7]], axis=0)
    lower = jnp.concatenate([stale[1:], sent[0:1, :, D + 2 * LANES :]], axis=0)
    column = lax.broadcasted_iota(jnp.int32, (QUERIES, LANES), 0) % COLS
    total = jnp.zeros((QUERIES, CO), F32)
    for dy, source in enumerate((upper, active, lower)):
        rows = source.reshape(QUERIES, LANES).astype(F32)
        left = jnp.where(column == 0, 0.0, pltpu.roll(rows, 1, 0))
        right = jnp.where(column == COLS - 1, 0.0, pltpu.roll(rows, QUERIES - 1, 0))
        three = jnp.concatenate([left.astype(BF16), rows.astype(BF16), right.astype(BF16)], axis=1)
        total += dot(dot(three, spread).astype(BF16), weights[dy])
    return total


def attend_kernel(sent, all_keys, all_values, gathered, other, after, back):
    del after
    z, j = place()
    rows = lax.broadcasted_iota(jnp.int32, (2 * QUERIES, LANES), 0)
    here = lax.broadcasted_iota(jnp.int32, (2 * QUERIES, LANES), 1) == 0
    own_query = jnp.where(here & (((rows // COLS) % GROUP) == j), -1e30, 0.0).astype(BF16)
    own_key = jnp.where(here & ((rows // COLS) == z), 1.0, 0.0).astype(BF16)
    masked = (own_query, own_key)
    lanes = lane_ids(QUERIES)
    low = lanes < HEAD_DIM
    stats = jnp.zeros((QUERIES, LANES), F32)
    for pair in range(PAIRS):
        at = slice(pair * LANES, (pair + 1) * LANES)
        query = sent[:, :, at].reshape(QUERIES, LANES)
        keys, values = all_keys[:, at], all_values[:, at]
        row_max, row_sum, weighted = attend_pair(query, keys, values, masked, lanes)
        mixed = jnp.where(low, weighted[:QUERIES], weighted[QUERIES:]) / jnp.where(
            low, row_sum[:QUERIES], row_sum[QUERIES:]
        )
        back[:, :, at] = mixed.astype(BF16).reshape(GROUP, COLS, LANES)
        for half in range(2):
            head = 2 * pair + half
            at_rows = slice(half * QUERIES, (half + 1) * QUERIES)
            stats = jnp.where(lanes == head, row_max[at_rows], stats)
            stats = jnp.where(lanes == HEADS + head, row_sum[at_rows], stats)
    high = stats.astype(BF16).astype(F32)
    rest = stats - high
    middle = rest.astype(BF16).astype(F32)
    last = rest - middle
    packed = sum(pltpu.roll(term, at, 1) for term, at in zip((high, middle, last), STATS_AT))
    total = convolve(sent, gathered, other)
    back[:, :, D : D + 2 * LANES] = (
        total[:, : 2 * LANES].astype(BF16).reshape(GROUP, COLS, 2 * LANES)
    )
    tail = jnp.concatenate([total[:, 2 * LANES :], packed[:, CO - 2 * LANES :]], axis=1)
    back[:, :, D + 2 * LANES :] = tail.astype(BF16).reshape(GROUP, COLS, LANES)


def fresh_kernel(own_keys, own_values, query, weighted_out, stats_out):
    lanes = lane_ids(COLS)
    low = lanes < HEAD_DIM
    stats = jnp.zeros((COLS, LANES), F32)
    for pair in range(PAIRS):
        at = slice(pair * LANES, (pair + 1) * LANES)
        row_max, row_sum, weighted = attend_pair(
            query[:, at], own_keys[:, at], own_values[:, at], None, lanes
        )
        weighted_out[:, at] = jnp.where(low, weighted[:COLS], weighted[COLS:])
        for half in range(2):
            head = 2 * pair + half
            at_rows = slice(half * COLS, (half + 1) * COLS)
            stats = jnp.where(lanes == head, row_max[at_rows], stats)
            stats = jnp.where(lanes == HEADS + head, row_sum[at_rows], stats)
    stats_out[...] = stats


def finish_kernel(partial, fresh, fresh_stats, wo, attended, convolved):
    total = jnp.zeros((COLS, CO), F32)
    for d in range(GROUP):
        total += partial[d, :, D : D + CO].astype(F32)
    convolved[...] = total.astype(BF16)
    stats = []
    for d in range(GROUP):
        packed = partial[d, :, D + 2 * LANES :].astype(F32)
        terms = sum(pltpu.roll(packed, LANES - at, 1) for at in STATS_AT)
        stats.append(jnp.where(lane_ids(COLS) < 2 * HEADS, terms, 0.0))
    stats.append(fresh_stats[...])
    top = stats[0]
    for s in stats[1:]:
        top = jnp.maximum(top, s)
    scale = [jnp.exp(s - top) for s in stats]
    sums = [pltpu.roll(s, LANES - HEADS, 1) for s in stats]
    parts = [scale[d] * sums[d] for d in range(GROUP)]
    whole = scale[GROUP] * sums[GROUP]
    for p in parts:
        whole = whole + p
    share = 1.0 / whole
    weights = [p * share for p in parts] + [scale[GROUP] * share]
    low = lane_ids(COLS) < HEAD_DIM
    mixed = []
    for pair in range(PAIRS):
        at = slice(pair * LANES, (pair + 1) * LANES)
        sum_pair = jnp.zeros((COLS, LANES), F32)
        for d in range(GROUP + 1):
            w = jnp.where(
                low, weights[d][:, 2 * pair : 2 * pair + 1], weights[d][:, 2 * pair + 1 : 2 * pair + 2]
            )
            sum_pair += w * (partial[d, :, at].astype(F32) if d < GROUP else fresh[:, at])
        mixed.append(sum_pair.astype(BF16))
    attended[...] = dot(jnp.concatenate(mixed, axis=1), wo[...]).astype(BF16)


ANY_SPEC = pl.BlockSpec(memory_space=pl.ANY)
VMEM_SPEC = pl.BlockSpec(memory_space=pltpu.VMEM)
HBM_SPEC = pl.BlockSpec(memory_space=pltpu.HBM)


def params():
    return pltpu.CompilerParams(vmem_limit_bytes=VMEM)


def cost(us):
    return pl.CostEstimate(flops=int(us * 1e9), bytes_accessed=0, transcendentals=0)


def shape(dims, dtype=BF16):
    return jax.ShapeDtypeStruct(dims, dtype)


def local(block_input, stale_input, query_weight, key_weight, value_weight, out_weight, conv_weight):
    block = block_input.reshape(COLS, D)
    stale = stale_input.reshape(COLS, D)
    with jax.named_scope("ahead"):
        ahead = pl.pallas_call(
            ahead_kernel,
            out_shape=shape((8, LANES), F32),
            compiler_params=params(),
            cost_estimate=cost(AHEAD),
        )()
    with jax.named_scope("payload"):
        payload = pl.pallas_call(
            payload_kernel,
            out_shape=shape((COLS + 16, D)),
            in_specs=[HBM_SPEC] * 2 + [ANY_SPEC],
            scratch_shapes=[
                pltpu.VMEM((COLS, D), BF16),
                pltpu.VMEM((9, OWN, CO), BF16),
                pltpu.VMEM((16, D), F32),
                pltpu.SemaphoreType.DMA((2,)),
            ],
            compiler_params=params(),
            cost_estimate=cost(PAYLOAD),
        )(stale, conv_weight, ahead)
    gathered = lax.all_gather(payload, "z", axis=0)
    with jax.named_scope("prepare"):
        send, query = pl.pallas_call(
            prepare_kernel,
            out_shape=(shape((GROUP, COLS, SEND)), shape((COLS, D))),
            compiler_params=params(),
            cost_estimate=cost(PREPARE),
        )(block, gathered, query_weight, jnp.asarray(slice_matrix()))
    sent = lax.all_to_all(send, ("yh", "x"), 0, 0, tiled=True)
    other = lax.ppermute(gathered[:, COLS:, :], "core", [(0, 1), (1, 0)])
    sides = []
    for name, weight in (("keys", key_weight), ("values", value_weight)):
        with jax.named_scope(name):
            sides.append(
                pl.pallas_call(
                    project_kernel,
                    out_shape=(shape((KEYS, D)), shape((COLS, D))),
                    in_specs=[VMEM_SPEC] * 3 + [ANY_SPEC],
                    compiler_params=params(),
                    cost_estimate=cost(PROJECT),
                )(gathered, block, weight, sides[0][0] if sides else send)
            )
    (keys, own_keys), (values, own_values) = sides
    with jax.named_scope("fresh"):
        fresh, fresh_stats = pl.pallas_call(
            fresh_kernel,
            out_shape=(shape((COLS, D), F32), shape((COLS, LANES), F32)),
            compiler_params=params(),
            cost_estimate=cost(FRESH),
        )(own_keys, own_values, query)
    with jax.named_scope("attend"):
        back = pl.pallas_call(
            attend_kernel,
            out_shape=shape((GROUP, COLS, BACK)),
            in_specs=[VMEM_SPEC] * 5 + [ANY_SPEC],
            compiler_params=params(),
            cost_estimate=cost(ATTEND),
        )(sent, keys, values, gathered, other, fresh_stats)
    partial = lax.all_to_all(back, ("yh", "x"), 0, 0, tiled=True)
    with jax.named_scope("finish"):
        attended, convolved = pl.pallas_call(
            finish_kernel,
            out_shape=(shape((COLS, D)), shape((COLS, CO))),
            compiler_params=params(),
            cost_estimate=cost(FINISH),
        )(partial, fresh, fresh_stats, out_weight)
    return attended.reshape(1, COLS, D), convolved.reshape(1, COLS, CO)


def solution(mesh):
    axes = Mesh(mesh.devices.reshape(Z, 2, 4, 2, 2), ("z", "yh", "x", "yl", "core"))
    rows, batch = ("z", "yh", "x"), ("yl", "core")
    placed = P(rows, batch, None)
    return jax.shard_map(
        local,
        mesh=axes,
        in_specs=(placed, placed, P(), P(), P(), P(), P(None, rows, None)),
        out_specs=(placed, placed),
        check_vma=False,
    )
```

```python
import jax
import jax.numpy as jnp
import ml_dtypes
import numpy as np
from jax import lax
from jax.experimental import pallas as pl
from jax.experimental.pallas import tpu as pltpu
from jax.sharding import Mesh, PartitionSpec as P

HEADS = 10
HEAD_DIM = 64
D = 640
CO = 320
COLS = 32
Z = 16
GROUP = 8
OWN = 5
LANES = 128
PAIRS = HEADS // 2
QUERIES = GROUP * COLS
KEYS = Z * COLS
SEND = D + 3 * LANES
BACK = D + 3 * LANES
VMEM = 24 * 1024 * 1024
PAYLOAD, PREPARE, PROJECT, ATTEND, FRESH, FINISH = 1, 2, 1, 3, 0.2, 2
AHEAD = 3
STATS_AT = (64, 84, 104)
F32 = jnp.float32
BF16 = jnp.bfloat16


def slice_matrix():
    out = np.zeros((D, GROUP * LANES), np.float32)
    for j in range(GROUP):
        for z in range(Z):
            for c in range(OWN):
                out[(z * GROUP + j) * OWN + c, LANES * j + 8 * z + c] = 1.0
    return out.astype(ml_dtypes.bfloat16)


def tap_matrix():
    row = lax.broadcasted_iota(jnp.int32, (3 * LANES, 2 * LANES), 0)
    col = lax.broadcasted_iota(jnp.int32, (3 * LANES, 2 * LANES), 1)
    z, c = (row % LANES) // 8, row % 8
    target = 16 * z + OWN * (row // LANES) + c
    return jnp.where((c < OWN) & (col == target), 1.0, 0.0).astype(BF16)


def layer_norm(values_in):
    mean = jnp.mean(values_in, axis=-1, keepdims=True)
    centered = values_in - mean
    variance = jnp.mean(centered * centered, axis=-1, keepdims=True)
    return (centered * lax.rsqrt(variance + 1e-05)).astype(BF16)


def silu(values_in):
    return (values_in * jax.nn.sigmoid(values_in)).astype(BF16)


def dot(a, b):
    return jnp.dot(a, b, preferred_element_type=F32)


def dot_t(a, b):
    return lax.dot_general(a, b, (((1,), (1,)), ((), ())), preferred_element_type=F32)


def lane_ids(rows):
    return lax.broadcasted_iota(jnp.int32, (rows, LANES), 1)


def place():
    return lax.axis_index("z"), lax.axis_index("yh") * 4 + lax.axis_index("x")


def ahead_kernel(out):
    out[...] = jnp.zeros_like(out)


def payload_kernel(stale_hbm, taps_hbm, after, gather, stale, taps, rows, sems):
    del after
    copies = [
        pltpu.make_async_copy(taps_hbm, taps, sems.at[0]),
        pltpu.make_async_copy(stale_hbm, stale, sems.at[1]),
    ]
    for copy in copies:
        copy.start()
    core = lax.axis_index("core")
    rows[...] = jnp.zeros_like(rows)
    copies[0].wait()
    for dx in range(3):
        first = jnp.where(core == 0, taps[dx].astype(F32), taps[6 + dx].astype(F32))
        second = jnp.where(core == 0, taps[3 + dx].astype(F32), 0.0)
        rows[OWN * dx : OWN * (dx + 1), :] = jnp.concatenate([first, second], axis=1)
    gather[COLS:, :] = rows[...].astype(BF16)
    copies[1].wait()
    gather[:COLS, :] = stale[...]


def prepare_kernel(block, gathered, wq, slices, send, query_out):
    z, j = place()
    beside = jnp.where(j == 0, jnp.minimum(z + 1, Z - 1), jnp.maximum(z - 1, 0))
    stale = gathered[z, :COLS, :]
    query = dot(layer_norm(block[...].astype(F32)), wq[...]).astype(BF16)
    query = query * jnp.array(HEAD_DIM**-0.5, BF16)
    query_out[...] = query
    outside = ((j == 0) & (z == Z - 1)) | ((j != 0) & (z == 0))
    halo = gathered[beside, :COLS, :].astype(F32) * jnp.where(outside, 0.0, 1.0)
    three = jnp.concatenate(
        [silu(block[...].astype(F32)), silu(stale.astype(F32)), silu(halo)], axis=0
    )
    cut = dot(three, slices[...]).astype(BF16)
    for j in range(GROUP):
        send[j, :, :D] = query
        for part in range(3):
            send[j, :, D + part * LANES : D + (part + 1) * LANES] = cut[
                part * COLS : (part + 1) * COLS, j * LANES : (j + 1) * LANES
            ]


def project_kernel(gathered, block, weight, after, out, own):
    del after
    rows = jnp.concatenate([gathered[:, :COLS, :].reshape(KEYS, D), block[...]], axis=0)
    projected = dot(layer_norm(rows.astype(F32)), weight[...]).astype(BF16)
    out[...] = projected[:KEYS]
    own[...] = projected[KEYS:]


def attend_pair(query, keys, values, masked, lanes):
    low = lanes < HEAD_DIM
    zero = jnp.zeros_like(query)
    two = jnp.concatenate([jnp.where(low, query, zero), jnp.where(low, zero, query)], axis=0)
    if masked is not None:
        two = jnp.concatenate([two, masked[0]], axis=1)
        keys = jnp.concatenate([keys, masked[1]], axis=1)
    scores = dot_t(two, keys)
    row_max = jnp.max(scores, axis=-1, keepdims=True)
    exp_scores = jnp.exp(scores - row_max)
    row_sum = jnp.sum(exp_scores, axis=-1, keepdims=True)
    weighted = dot(exp_scores.astype(BF16), values)
    return row_max, row_sum, weighted


def convolve(sent, gathered, other):
    spread = tap_matrix()
    mine = gathered[:, COLS:, :].reshape(Z * 16, D)
    theirs = other[...].reshape(Z * 16, D)
    zero_core = lax.axis_index("core") == 0
    lower_half = jnp.where(zero_core, mine, theirs)
    upper_half = jnp.where(zero_core, theirs, mine)
    weights = (lower_half[:, :CO], lower_half[:, CO:], upper_half[:, :CO])
    active = sent[:, :, D : D + LANES]
    stale = sent[:, :, D + LANES : D + 2 * LANES]
    upper = jnp.concatenate([sent[7:8, :, D + 2 * LANES :], stale[:7]], axis=0)
    lower = jnp.concatenate([stale[1:], sent[0:1, :, D + 2 * LANES :]], axis=0)
    column = lax.broadcasted_iota(jnp.int32, (QUERIES, LANES), 0) % COLS
    total = jnp.zeros((QUERIES, CO), F32)
    for dy, source in enumerate((upper, active, lower)):
        rows = source.reshape(QUERIES, LANES).astype(F32)
        left = jnp.where(column == 0, 0.0, pltpu.roll(rows, 1, 0))
        right = jnp.where(column == COLS - 1, 0.0, pltpu.roll(rows, QUERIES - 1, 0))
        three = jnp.concatenate([left.astype(BF16), rows.astype(BF16), right.astype(BF16)], axis=1)
        total += dot(dot(three, spread).astype(BF16), weights[dy])
    return total


def attend_kernel(sent, all_keys, all_values, gathered, other, after, back):
    del after
    z, j = place()
    rows = lax.broadcasted_iota(jnp.int32, (2 * QUERIES, LANES), 0)
    here = lax.broadcasted_iota(jnp.int32, (2 * QUERIES, LANES), 1) == 0
    own_query = jnp.where(here & (((rows // COLS) % GROUP) == j), -1e30, 0.0).astype(BF16)
    own_key = jnp.where(here & ((rows // COLS) == z), 1.0, 0.0).astype(BF16)
    masked = (own_query, own_key)
    lanes = lane_ids(QUERIES)
    low = lanes < HEAD_DIM
    stats = jnp.zeros((QUERIES, LANES), F32)
    for pair in range(PAIRS):
        at = slice(pair * LANES, (pair + 1) * LANES)
        query = sent[:, :, at].reshape(QUERIES, LANES)
        keys, values = all_keys[:, at], all_values[:, at]
        row_max, row_sum, weighted = attend_pair(query, keys, values, masked, lanes)
        mixed = jnp.where(low, weighted[:QUERIES], weighted[QUERIES:]) / jnp.where(
            low, row_sum[:QUERIES], row_sum[QUERIES:]
        )
        back[:, :, at] = mixed.astype(BF16).reshape(GROUP, COLS, LANES)
        for half in range(2):
            head = 2 * pair + half
            at_rows = slice(half * QUERIES, (half + 1) * QUERIES)
            stats = jnp.where(lanes == head, row_max[at_rows], stats)
            stats = jnp.where(lanes == HEADS + head, row_sum[at_rows], stats)
    high = stats.astype(BF16).astype(F32)
    rest = stats - high
    middle = rest.astype(BF16).astype(F32)
    last = rest - middle
    packed = sum(pltpu.roll(term, at, 1) for term, at in zip((high, middle, last), STATS_AT))
    total = convolve(sent, gathered, other)
    back[:, :, D : D + 2 * LANES] = (
        total[:, : 2 * LANES].astype(BF16).reshape(GROUP, COLS, 2 * LANES)
    )
    tail = jnp.concatenate([total[:, 2 * LANES :], packed[:, CO - 2 * LANES :]], axis=1)
    back[:, :, D + 2 * LANES :] = tail.astype(BF16).reshape(GROUP, COLS, LANES)


def fresh_kernel(own_keys, own_values, query, weighted_out, stats_out):
    lanes = lane_ids(COLS)
    low = lanes < HEAD_DIM
    stats = jnp.zeros((COLS, LANES), F32)
    for pair in range(PAIRS):
        at = slice(pair * LANES, (pair + 1) * LANES)
        row_max, row_sum, weighted = attend_pair(
            query[:, at], own_keys[:, at], own_values[:, at], None, lanes
        )
        weighted_out[:, at] = jnp.where(low, weighted[:COLS], weighted[COLS:])
        for half in range(2):
            head = 2 * pair + half
            at_rows = slice(half * COLS, (half + 1) * COLS)
            stats = jnp.where(lanes == head, row_max[at_rows], stats)
            stats = jnp.where(lanes == HEADS + head, row_sum[at_rows], stats)
    stats_out[...] = stats


def finish_kernel(partial, fresh, fresh_stats, wo, attended, convolved):
    total = jnp.zeros((COLS, CO), F32)
    for d in range(GROUP):
        total += partial[d, :, D : D + CO].astype(F32)
    convolved[...] = total.astype(BF16)
    stats = []
    for d in range(GROUP):
        packed = partial[d, :, D + 2 * LANES :].astype(F32)
        terms = sum(pltpu.roll(packed, LANES - at, 1) for at in STATS_AT)
        stats.append(jnp.where(lane_ids(COLS) < 2 * HEADS, terms, 0.0))
    stats.append(fresh_stats[...])
    top = stats[0]
    for s in stats[1:]:
        top = jnp.maximum(top, s)
    scale = [jnp.exp(s - top) for s in stats]
    sums = [pltpu.roll(s, LANES - HEADS, 1) for s in stats]
    parts = [scale[d] * sums[d] for d in range(GROUP)]
    whole = scale[GROUP] * sums[GROUP]
    for p in parts:
        whole = whole + p
    share = 1.0 / whole
    weights = [p * share for p in parts] + [scale[GROUP] * share]
    low = lane_ids(COLS) < HEAD_DIM
    mixed = []
    for pair in range(PAIRS):
        at = slice(pair * LANES, (pair + 1) * LANES)
        sum_pair = jnp.zeros((COLS, LANES), F32)
        for d in range(GROUP + 1):
            w = jnp.where(
                low, weights[d][:, 2 * pair : 2 * pair + 1], weights[d][:, 2 * pair + 1 : 2 * pair + 2]
            )
            sum_pair += w * (partial[d, :, at].astype(F32) if d < GROUP else fresh[:, at])
        mixed.append(sum_pair.astype(BF16))
    attended[...] = dot(jnp.concatenate(mixed, axis=1), wo[...]).astype(BF16)


ANY_SPEC = pl.BlockSpec(memory_space=pl.ANY)
VMEM_SPEC = pl.BlockSpec(memory_space=pltpu.VMEM)
HBM_SPEC = pl.BlockSpec(memory_space=pltpu.HBM)


def params():
    return pltpu.CompilerParams(vmem_limit_bytes=VMEM)


def cost(us):
    return pl.CostEstimate(flops=int(us * 1e9), bytes_accessed=0, transcendentals=0)


def shape(dims, dtype=BF16):
    return jax.ShapeDtypeStruct(dims, dtype)


def local(block_input, stale_input, query_weight, key_weight, value_weight, out_weight, conv_weight):
    block = block_input.reshape(COLS, D)
    stale = stale_input.reshape(COLS, D)
    with jax.named_scope("ahead"):
        ahead = pl.pallas_call(
            ahead_kernel,
            out_shape=shape((8, LANES), F32),
            compiler_params=params(),
            cost_estimate=cost(AHEAD),
        )()
    with jax.named_scope("payload"):
        payload = pl.pallas_call(
            payload_kernel,
            out_shape=shape((COLS + 16, D)),
            in_specs=[HBM_SPEC] * 2 + [ANY_SPEC],
            scratch_shapes=[
                pltpu.VMEM((COLS, D), BF16),
                pltpu.VMEM((9, OWN, CO), BF16),
                pltpu.VMEM((16, D), F32),
                pltpu.SemaphoreType.DMA((2,)),
            ],
            compiler_params=params(),
            cost_estimate=cost(PAYLOAD),
        )(stale, conv_weight, ahead)
    gathered = lax.all_gather(payload, "z", axis=0)
    with jax.named_scope("prepare"):
        send, query = pl.pallas_call(
            prepare_kernel,
            out_shape=(shape((GROUP, COLS, SEND)), shape((COLS, D))),
            compiler_params=params(),
            cost_estimate=cost(PREPARE),
        )(block, gathered, query_weight, jnp.asarray(slice_matrix()))
    sent = lax.all_to_all(send, ("yh", "x"), 0, 0, tiled=True)
    other = lax.ppermute(gathered[:, COLS:, :], "core", [(0, 1), (1, 0)])
    sides = []
    for name, weight in (("keys", key_weight), ("values", value_weight)):
        with jax.named_scope(name):
            sides.append(
                pl.pallas_call(
                    project_kernel,
                    out_shape=(shape((KEYS, D)), shape((COLS, D))),
                    in_specs=[VMEM_SPEC] * 3 + [ANY_SPEC],
                    compiler_params=params(),
                    cost_estimate=cost(PROJECT),
                )(gathered, block, weight, sides[0][0] if sides else send)
            )
    (keys, own_keys), (values, own_values) = sides
    with jax.named_scope("fresh"):
        fresh, fresh_stats = pl.pallas_call(
            fresh_kernel,
            out_shape=(shape((COLS, D), F32), shape((COLS, LANES), F32)),
            compiler_params=params(),
            cost_estimate=cost(FRESH),
        )(own_keys, own_values, query)
    with jax.named_scope("attend"):
        back = pl.pallas_call(
            attend_kernel,
            out_shape=shape((GROUP, COLS, BACK)),
            in_specs=[VMEM_SPEC] * 5 + [ANY_SPEC],
            compiler_params=params(),
            cost_estimate=cost(ATTEND),
        )(sent, keys, values, gathered, other, fresh_stats)
    partial = lax.all_to_all(back, ("yh", "x"), 0, 0, tiled=True)
    with jax.named_scope("finish"):
        attended, convolved = pl.pallas_call(
            finish_kernel,
            out_shape=(shape((COLS, D)), shape((COLS, CO))),
            compiler_params=params(),
            cost_estimate=cost(FINISH),
        )(partial, fresh, fresh_stats, out_weight)
    return attended.reshape(1, COLS, D), convolved.reshape(1, COLS, CO)


def solution(mesh):
    axes = Mesh(mesh.devices.reshape(Z, 2, 4, 2, 2), ("z", "yh", "x", "yl", "core"))
    rows, batch = ("z", "yh", "x"), ("yl", "core")
    placed = P(rows, batch, None)
    return jax.shard_map(
        local,
        mesh=axes,
        in_specs=(placed, placed, P(), P(), P(), P(), P(None, rows, None)),
        out_specs=(placed, placed),
        check_vma=False,
    )
```

```python
import jax
import jax.numpy as jnp
import ml_dtypes
import numpy as np
from jax import lax
from jax.experimental import pallas as pl
from jax.experimental.pallas import tpu as pltpu
from jax.sharding import Mesh, PartitionSpec as P

HEADS = 10
HEAD_DIM = 64
D = 640
CO = 320
COLS = 32
Z = 16
GROUP = 8
OWN = 5
LANES = 128
PAIRS = HEADS // 2
QUERIES = GROUP * COLS
KEYS = Z * COLS
SLICE = Z * OWN
FREE = LANES - SLICE
SEND = D + 2 * LANES
BACK = D + 3 * LANES
VMEM = 24 * 1024 * 1024
PAYLOAD, PREPARE, PROJECT, ATTEND, FRESH, FINISH = 1, 2, 1, 3, 0.2, 2
AHEAD = 3
STATS_AT = (64, 84, 104)
F32 = jnp.float32
BF16 = jnp.bfloat16


def slice_matrix():
    out = np.zeros((D, GROUP * LANES), np.float32)
    for j in range(GROUP):
        for z in range(Z):
            for c in range(OWN):
                out[(z * GROUP + j) * OWN + c, LANES * j + OWN * z + c] = 1.0
    return out.astype(ml_dtypes.bfloat16)


def tap_matrix():
    row = lax.broadcasted_iota(jnp.int32, (3 * LANES, 2 * LANES), 0)
    col = lax.broadcasted_iota(jnp.int32, (3 * LANES, 2 * LANES), 1)
    lane = row % LANES
    z, tap = col // 16, col % 16 - OWN * (row // LANES)
    hit = (tap >= 0) & (tap < OWN) & (lane == OWN * z + tap) & (lane < SLICE)
    return jnp.where(hit, 1.0, 0.0).astype(BF16)


def layer_norm(values_in):
    mean = jnp.mean(values_in, axis=-1, keepdims=True)
    centered = values_in - mean
    variance = jnp.mean(centered * centered, axis=-1, keepdims=True)
    return (centered * lax.rsqrt(variance + 1e-05)).astype(BF16)


def silu(values_in):
    return (values_in * jax.nn.sigmoid(values_in)).astype(BF16)


def dot(a, b):
    return jnp.dot(a, b, preferred_element_type=F32)


def dot_t(a, b):
    return lax.dot_general(a, b, (((1,), (1,)), ((), ())), preferred_element_type=F32)


def lane_ids(rows):
    return lax.broadcasted_iota(jnp.int32, (rows, LANES), 1)


def place():
    return lax.axis_index("z"), lax.axis_index("yh") * 4 + lax.axis_index("x")


def ahead_kernel(out):
    out[...] = jnp.zeros_like(out)


def payload_kernel(stale_hbm, taps_hbm, after, gather, stale, taps, rows, sems):
    del after
    copies = [
        pltpu.make_async_copy(taps_hbm, taps, sems.at[0]),
        pltpu.make_async_copy(stale_hbm, stale, sems.at[1]),
    ]
    for copy in copies:
        copy.start()
    core = lax.axis_index("core")
    rows[...] = jnp.zeros_like(rows)
    copies[0].wait()
    for dx in range(3):
        first = jnp.where(core == 0, taps[dx].astype(F32), taps[6 + dx].astype(F32))
        second = jnp.where(core == 0, taps[3 + dx].astype(F32), 0.0)
        rows[OWN * dx : OWN * (dx + 1), :] = jnp.concatenate([first, second], axis=1)
    gather[COLS:, :] = rows[...].astype(BF16)
    copies[1].wait()
    gather[:COLS, :] = stale[...]


def prepare_kernel(block, gathered, wq, slices, send, query_out):
    z, j = place()
    beside = jnp.where(j == 0, jnp.minimum(z + 1, Z - 1), jnp.maximum(z - 1, 0))
    stale = gathered[z, :COLS, :]
    query = dot(layer_norm(block[...].astype(F32)), wq[...]).astype(BF16)
    query = query * jnp.array(HEAD_DIM**-0.5, BF16)
    query_out[...] = query
    outside = ((j == 0) & (z == Z - 1)) | ((j != 0) & (z == 0))
    halo = gathered[beside, :COLS, :].astype(F32) * jnp.where(outside, 0.0, 1.0)
    three = jnp.concatenate(
        [silu(block[...].astype(F32)), silu(stale.astype(F32)), silu(halo)], axis=0
    )
    cut = dot(three, slices[...])
    lanes = lane_ids(COLS)
    for to in range(GROUP):
        at = slice(to * LANES, (to + 1) * LANES)
        active, before, rim = (cut[part * COLS : (part + 1) * COLS, at] for part in range(3))
        send[to, :, :D] = query
        send[to, :, D : D + LANES] = jnp.where(
            lanes < SLICE, active, pltpu.roll(rim, SLICE, 1)
        ).astype(BF16)
        send[to, :, D + LANES :] = jnp.where(
            lanes < SLICE, before, pltpu.roll(rim, SLICE - FREE, 1)
        ).astype(BF16)


def project_kernel(gathered, block, weight, after, out, own):
    del after
    rows = jnp.concatenate([gathered[:, :COLS, :].reshape(KEYS, D), block[...]], axis=0)
    projected = dot(layer_norm(rows.astype(F32)), weight[...]).astype(BF16)
    out[...] = projected[:KEYS]
    own[...] = projected[KEYS:]


def attend_pair(query, keys, values, masked, lanes):
    low = lanes < HEAD_DIM
    zero = jnp.zeros_like(query)
    two = jnp.concatenate([jnp.where(low, query, zero), jnp.where(low, zero, query)], axis=0)
    if masked is not None:
        two = jnp.concatenate([two, masked[0]], axis=1)
        keys = jnp.concatenate([keys, masked[1]], axis=1)
    scores = dot_t(two, keys)
    row_max = jnp.max(scores, axis=-1, keepdims=True)
    exp_scores = jnp.exp(scores - row_max)
    row_sum = jnp.sum(exp_scores, axis=-1, keepdims=True)
    weighted = dot(exp_scores.astype(BF16), values)
    return row_max, row_sum, weighted


def convolve(sent, gathered, other):
    spread = tap_matrix()
    mine = gathered[:, COLS:, :].reshape(Z * 16, D)
    theirs = other[...].reshape(Z * 16, D)
    zero_core = lax.axis_index("core") == 0
    lower_half = jnp.where(zero_core, mine, theirs)
    upper_half = jnp.where(zero_core, theirs, mine)
    weights = (lower_half[:, :CO], lower_half[:, CO:], upper_half[:, :CO])
    active = sent[:, :, D : D + LANES]
    stale = sent[:, :, D + LANES :]

    def rim(member):
        first = pltpu.roll(active[member].astype(F32), FREE, 1)
        rest = pltpu.roll(stale[member].astype(F32), LANES - (SLICE - FREE), 1)
        return jnp.where(lane_ids(COLS) < FREE, first, rest).astype(BF16)[None]

    upper = jnp.concatenate([rim(GROUP - 1), stale[:7]], axis=0)
    lower = jnp.concatenate([stale[1:], rim(0)], axis=0)
    column = lax.broadcasted_iota(jnp.int32, (QUERIES, LANES), 0) % COLS
    total = jnp.zeros((QUERIES, CO), F32)
    for dy, source in enumerate((upper, active, lower)):
        rows = source.reshape(QUERIES, LANES).astype(F32)
        left = jnp.where(column == 0, 0.0, pltpu.roll(rows, 1, 0))
        right = jnp.where(column == COLS - 1, 0.0, pltpu.roll(rows, QUERIES - 1, 0))
        three = jnp.concatenate([left.astype(BF16), rows.astype(BF16), right.astype(BF16)], axis=1)
        total += dot(dot(three, spread).astype(BF16), weights[dy])
    return total


def attend_kernel(sent, all_keys, all_values, gathered, other, after, back):
    del after
    z, j = place()
    rows = lax.broadcasted_iota(jnp.int32, (2 * QUERIES, LANES), 0)
    here = lax.broadcasted_iota(jnp.int32, (2 * QUERIES, LANES), 1) == 0
    own_query = jnp.where(here & (((rows // COLS) % GROUP) == j), -1e30, 0.0).astype(BF16)
    own_key = jnp.where(here & ((rows // COLS) == z), 1.0, 0.0).astype(BF16)
    masked = (own_query, own_key)
    lanes = lane_ids(QUERIES)
    low = lanes < HEAD_DIM
    stats = jnp.zeros((QUERIES, LANES), F32)
    for pair in range(PAIRS):
        at = slice(pair * LANES, (pair + 1) * LANES)
        query = sent[:, :, at].reshape(QUERIES, LANES)
        keys, values = all_keys[:, at], all_values[:, at]
        row_max, row_sum, weighted = attend_pair(query, keys, values, masked, lanes)
        mixed = jnp.where(low, weighted[:QUERIES], weighted[QUERIES:]) / jnp.where(
            low, row_sum[:QUERIES], row_sum[QUERIES:]
        )
        back[:, :, at] = mixed.astype(BF16).reshape(GROUP, COLS, LANES)
        for half in range(2):
            head = 2 * pair + half
            at_rows = slice(half * QUERIES, (half + 1) * QUERIES)
            stats = jnp.where(lanes == head, row_max[at_rows], stats)
            stats = jnp.where(lanes == HEADS + head, row_sum[at_rows], stats)
    high = stats.astype(BF16).astype(F32)
    rest = stats - high
    middle = rest.astype(BF16).astype(F32)
    last = rest - middle
    packed = sum(pltpu.roll(term, at, 1) for term, at in zip((high, middle, last), STATS_AT))
    total = convolve(sent, gathered, other)
    back[:, :, D : D + 2 * LANES] = (
        total[:, : 2 * LANES].astype(BF16).reshape(GROUP, COLS, 2 * LANES)
    )
    tail = jnp.concatenate([total[:, 2 * LANES :], packed[:, CO - 2 * LANES :]], axis=1)
    back[:, :, D + 2 * LANES :] = tail.astype(BF16).reshape(GROUP, COLS, LANES)


def fresh_kernel(own_keys, own_values, query, weighted_out, stats_out):
    lanes = lane_ids(COLS)
    low = lanes < HEAD_DIM
    stats = jnp.zeros((COLS, LANES), F32)
    for pair in range(PAIRS):
        at = slice(pair * LANES, (pair + 1) * LANES)
        row_max, row_sum, weighted = attend_pair(
            query[:, at], own_keys[:, at], own_values[:, at], None, lanes
        )
        weighted_out[:, at] = jnp.where(low, weighted[:COLS], weighted[COLS:])
        for half in range(2):
            head = 2 * pair + half
            at_rows = slice(half * COLS, (half + 1) * COLS)
            stats = jnp.where(lanes == head, row_max[at_rows], stats)
            stats = jnp.where(lanes == HEADS + head, row_sum[at_rows], stats)
    stats_out[...] = stats


def finish_kernel(partial, fresh, fresh_stats, wo, attended, convolved):
    total = jnp.zeros((COLS, CO), F32)
    for d in range(GROUP):
        total += partial[d, :, D : D + CO].astype(F32)
    convolved[...] = total.astype(BF16)
    stats = []
    for d in range(GROUP):
        packed = partial[d, :, D + 2 * LANES :].astype(F32)
        terms = sum(pltpu.roll(packed, LANES - at, 1) for at in STATS_AT)
        stats.append(jnp.where(lane_ids(COLS) < 2 * HEADS, terms, 0.0))
    stats.append(fresh_stats[...])
    top = stats[0]
    for s in stats[1:]:
        top = jnp.maximum(top, s)
    scale = [jnp.exp(s - top) for s in stats]
    sums = [pltpu.roll(s, LANES - HEADS, 1) for s in stats]
    parts = [scale[d] * sums[d] for d in range(GROUP)]
    whole = scale[GROUP] * sums[GROUP]
    for p in parts:
        whole = whole + p
    share = 1.0 / whole
    weights = [p * share for p in parts] + [scale[GROUP] * share]
    low = lane_ids(COLS) < HEAD_DIM
    mixed = []
    for pair in range(PAIRS):
        at = slice(pair * LANES, (pair + 1) * LANES)
        sum_pair = jnp.zeros((COLS, LANES), F32)
        for d in range(GROUP + 1):
            w = jnp.where(
                low, weights[d][:, 2 * pair : 2 * pair + 1], weights[d][:, 2 * pair + 1 : 2 * pair + 2]
            )
            sum_pair += w * (partial[d, :, at].astype(F32) if d < GROUP else fresh[:, at])
        mixed.append(sum_pair.astype(BF16))
    attended[...] = dot(jnp.concatenate(mixed, axis=1), wo[...]).astype(BF16)


ANY_SPEC = pl.BlockSpec(memory_space=pl.ANY)
VMEM_SPEC = pl.BlockSpec(memory_space=pltpu.VMEM)
HBM_SPEC = pl.BlockSpec(memory_space=pltpu.HBM)


def params():
    return pltpu.CompilerParams(vmem_limit_bytes=VMEM)


def cost(us):
    return pl.CostEstimate(flops=int(us * 1e9), bytes_accessed=0, transcendentals=0)


def shape(dims, dtype=BF16):
    return jax.ShapeDtypeStruct(dims, dtype)


def local(block_input, stale_input, query_weight, key_weight, value_weight, out_weight, conv_weight):
    block = block_input.reshape(COLS, D)
    stale = stale_input.reshape(COLS, D)
    with jax.named_scope("ahead"):
        ahead = pl.pallas_call(
            ahead_kernel,
            out_shape=shape((8, LANES), F32),
            compiler_params=params(),
            cost_estimate=cost(AHEAD),
        )()
    with jax.named_scope("payload"):
        payload = pl.pallas_call(
            payload_kernel,
            out_shape=shape((COLS + 16, D)),
            in_specs=[HBM_SPEC] * 2 + [ANY_SPEC],
            scratch_shapes=[
                pltpu.VMEM((COLS, D), BF16),
                pltpu.VMEM((9, OWN, CO), BF16),
                pltpu.VMEM((16, D), F32),
                pltpu.SemaphoreType.DMA((2,)),
            ],
            compiler_params=params(),
            cost_estimate=cost(PAYLOAD),
        )(stale, conv_weight, ahead)
    gathered = lax.all_gather(payload, "z", axis=0)
    with jax.named_scope("prepare"):
        send, query = pl.pallas_call(
            prepare_kernel,
            out_shape=(shape((GROUP, COLS, SEND)), shape((COLS, D))),
            compiler_params=params(),
            cost_estimate=cost(PREPARE),
        )(block, gathered, query_weight, jnp.asarray(slice_matrix()))
    sent = lax.all_to_all(send, ("yh", "x"), 0, 0, tiled=True)
    other = lax.ppermute(gathered[:, COLS:, :], "core", [(0, 1), (1, 0)])
    sides = []
    for name, weight in (("keys", key_weight), ("values", value_weight)):
        with jax.named_scope(name):
            sides.append(
                pl.pallas_call(
                    project_kernel,
                    out_shape=(shape((KEYS, D)), shape((COLS, D))),
                    in_specs=[VMEM_SPEC] * 3 + [ANY_SPEC],
                    compiler_params=params(),
                    cost_estimate=cost(PROJECT),
                )(gathered, block, weight, sides[0][0] if sides else send)
            )
    (keys, own_keys), (values, own_values) = sides
    with jax.named_scope("fresh"):
        fresh, fresh_stats = pl.pallas_call(
            fresh_kernel,
            out_shape=(shape((COLS, D), F32), shape((COLS, LANES), F32)),
            compiler_params=params(),
            cost_estimate=cost(FRESH),
        )(own_keys, own_values, query)
    with jax.named_scope("attend"):
        back = pl.pallas_call(
            attend_kernel,
            out_shape=shape((GROUP, COLS, BACK)),
            in_specs=[VMEM_SPEC] * 5 + [ANY_SPEC],
            compiler_params=params(),
            cost_estimate=cost(ATTEND),
        )(sent, keys, values, gathered, other, fresh_stats)
    partial = lax.all_to_all(back, ("yh", "x"), 0, 0, tiled=True)
    with jax.named_scope("finish"):
        attended, convolved = pl.pallas_call(
            finish_kernel,
            out_shape=(shape((COLS, D)), shape((COLS, CO))),
            compiler_params=params(),
            cost_estimate=cost(FINISH),
        )(partial, fresh, fresh_stats, out_weight)
    return attended.reshape(1, COLS, D), convolved.reshape(1, COLS, CO)


def solution(mesh):
    axes = Mesh(mesh.devices.reshape(Z, 2, 4, 2, 2), ("z", "yh", "x", "yl", "core"))
    rows, batch = ("z", "yh", "x"), ("yl", "core")
    placed = P(rows, batch, None)
    return jax.shard_map(
        local,
        mesh=axes,
        in_specs=(placed, placed, P(), P(), P(), P(), P(None, rows, None)),
        out_specs=(placed, placed),
        check_vma=False,
    )
```
